32 devices in a mesh: ctx: 8 (over z, x), tp: 4 (over y, core).
Axes of the slice: x: 2, y: 2, z: 4, core: 2. Of those that a mesh axis runs over, the one named last changes fastest.
Arguments:
- tokens: bfloat16 [2048, 4096], P(('ctx', 'tp')), may hold values from -6 to 6
- in_x: bfloat16 [4096, 4096], P(None, 'tp'), may hold values from -0.09375 to 0.09375
- in_bc: bfloat16 [4096, 256], replicated, may hold values from -0.09375 to 0.09375
- in_dt: bfloat16 [4096, 64], P(None, 'tp'), may hold values from -0.09375 to 0.09375
- conv_x: float32 [4, 4096], P(None, 'tp'), may hold values from -3 to 3
- conv_bc: float32 [4, 256], replicated, may hold values from -3 to 3
- dt_bias: float32 [64], P('tp'), may hold values from -7.5 to -3.5
- a_log: float32 [64], P('tp'), may hold values from -4.61 to 0.41
- skip_d: float32 [64], P('tp'), may hold values from 0.5 to 1.5
- norm_gain: float32 [4096], P('tp'), may hold values from 0.1 to 1.9
- out_w: bfloat16 [4096, 4096], P('tp'), may hold values from -0.09375 to 0.09375
Outputs:
- mixed: bfloat16 [2048, 4096], P(('ctx', 'tp'))
The draws below stay inside these ranges and needn't reach their ends.
All inputs are finite; a program needn't handle non-finite values.
Results may differ from the reference program's by a relative error of at most 0.019.
Values may be sent and summed in bfloat16 or wider, within the bound.
A program may use at most 64 MiB of HBM per device.

```python
import math
import jax
import jax.numpy as jnp
from jax import lax

D = 4096
HEADS = 64
HEAD_DIM = 64
STATE = 128
CONV = 4
BLOCK = 256
INNER = 4096
TOKENS = 2048


def head_kinds(key):
    pick_key = jax.random.fold_in(key, 11)
    share = 0.5
    return jax.random.uniform(pick_key, (HEADS,), jnp.float32) < share


def draw_a_log(key, part):
    fast = head_kinds(key)
    fast_key = jax.random.fold_in(key, 12)
    slow_key = jax.random.fold_in(key, 13)
    fast_vals = jax.random.uniform(fast_key, (HEADS,), jnp.float32, math.log(0.5), math.log(1.5))
    slow_vals = jax.random.uniform(slow_key, (HEADS,), jnp.float32, math.log(0.01), math.log(0.03))
    return jnp.where(fast, fast_vals, slow_vals).astype(jnp.float32)


def draw_dt_bias(key, part):
    fast = head_kinds(key)
    fast_key = jax.random.fold_in(key, 14)
    slow_key = jax.random.fold_in(key, 15)
    fast_vals = jax.random.uniform(fast_key, (HEADS,), jnp.float32, -4.5, -3.5)
    slow_vals = jax.random.uniform(slow_key, (HEADS,), jnp.float32, -7.5, -6.9)
    return jnp.where(fast, fast_vals, slow_vals).astype(jnp.float32)


def level_of(rng, dims, cuts, least, largest):
    def one(axis_at, parts):
        steps = jax.random.uniform(jax.random.fold_in(jax.random.fold_in(rng, 6), axis_at), (parts,), jnp.float32, least / len(cuts), largest / len(cuts))
        return jnp.repeat(jnp.exp(steps), dims[axis_at] // parts).reshape((-1,) + (1,) * (len(dims) - axis_at - 1))

    gain = one(*cuts[0])
    for cut in cuts[1:]:
        gain = gain * one(*cut)
    return gain


def bell_draw(stream_key, extent, deviation, most, shards=(), dtype=jnp.bfloat16):
    array = jax.random.normal(stream_key, extent, jnp.float32) * deviation
    if len(shards) > 0:
        array = level_of(stream_key, extent, shards, -0.22, 0.18) * array
    return jnp.clip(array, min=-most, max=most).astype(dtype)


def setup_inputs(seed: int = 0) -> dict:
    seeds = jax.random.split(jax.random.key(seed), 12)
    return {
        "tokens": bell_draw(seeds[0], (TOKENS, D), 1.0, 6.0, ((0, 32),)),
        "in_x": bell_draw(seeds[1], (D, INNER), D ** -0.5, 0.09375, ((1, 4),)),
        "in_bc": bell_draw(seeds[2], (D, 2 * STATE), D ** -0.5, 0.09375),
        "in_dt": bell_draw(seeds[3], (D, HEADS), D ** -0.5, 0.09375, ((1, 4),)),
        "conv_x": bell_draw(seeds[4], (CONV, INNER), CONV ** -0.5, 3.0, ((1, 4),), jnp.float32),
        "conv_bc": bell_draw(seeds[5], (CONV, 2 * STATE), CONV ** -0.5, 3.0, (), jnp.float32),
        "dt_bias": draw_dt_bias(jax.random.fold_in(seeds[11], 71), 0),
        "a_log": draw_a_log(jax.random.fold_in(seeds[11], 71), 0),
        "skip_d": jnp.clip(0.5 + 1.0 * jax.random.uniform(seeds[8], (HEADS,), jnp.float32) ** level_of(seeds[8], (HEADS,), ((0, 4),), -0.2, 0.2), 0.5, 1.5),
        "norm_gain": jnp.clip(1.0 + 0.18 * jax.random.normal(seeds[9], (INNER,), jnp.float32), 0.1, 1.9),
        "out_w": bell_draw(seeds[10], (INNER, D), INNER ** -0.5, 0.09375, ((0, 4),)),
    }


def causal_conv(prev, cur, kernel):
    ext = jnp.concatenate([prev, cur], 0).astype(jnp.float32)
    rows = cur.shape[0]
    taps = kernel.shape[0]
    total = kernel[0][None, :] * ext[0:rows]
    for k in range(1, taps):
        total = total + kernel[k][None, :] * ext[k:k + rows]
    return jax.nn.silu(total)

def ssd_block(state, xb, bb, cb, lab, dtb):
    hi = lax.Precision.HIGHEST
    length = lab.shape[0]
    cs = jnp.cumsum(lab, axis=0)
    scores = jnp.dot(cb, bb.T, precision=hi)
    diff = cs[:, None, :] - cs[None, :, :]
    later = lax.broadcasted_iota(jnp.int32, (length, length), 0)
    earlier = lax.broadcasted_iota(jnp.int32, (length, length), 1)
    tri = (later >= earlier)[:, :, None]
    decay = jnp.exp(jnp.where(tri, diff, -jnp.inf))
    xdt = xb * dtb[:, :, None]
    weighted = scores[:, :, None] * decay
    y_in = jnp.einsum('tsh,shp->thp', weighted, xdt, precision=hi)
    y_st = jnp.exp(cs)[:, :, None] * jnp.einsum('tn,hpn->thp', cb, state, precision=hi)
    tail = jnp.exp(cs[-1][None, :] - cs)
    fresh = jnp.einsum('shp,sn->hpn', xdt * tail[:, :, None], bb, precision=hi)
    new_state = jnp.exp(cs[-1])[:, None, None] * state + fresh
    return (new_state, y_in + y_st)

def reference(tokens, in_x, in_bc, in_dt, conv_x, conv_bc, dt_bias, a_log, skip_d, norm_gain, out_w):
    x_raw = jnp.dot(tokens, in_x, preferred_element_type=jnp.float32).astype(jnp.bfloat16)
    bc_raw = jnp.dot(tokens, in_bc, preferred_element_type=jnp.float32).astype(jnp.bfloat16)
    dt_raw = jnp.dot(tokens, in_dt, preferred_element_type=jnp.float32)
    x_conv = causal_conv(jnp.zeros((CONV - 1, INNER), jnp.bfloat16), x_raw, conv_x)
    bc_conv = causal_conv(jnp.zeros((CONV - 1, 2 * STATE), jnp.bfloat16), bc_raw, conv_bc)
    b_all = bc_conv[:, :STATE]
    c_all = bc_conv[:, STATE:]
    step_dt = jax.nn.softplus(dt_raw + dt_bias[None, :])
    log_decay = -jnp.exp(a_log)[None, :] * step_dt
    blocks = TOKENS // BLOCK
    x_heads = x_conv.reshape(blocks, BLOCK, HEADS, HEAD_DIM)

    def scan_step(state, inputs):
        xb, bb, cb, lab, dtb = inputs
        return ssd_block(state, xb, bb, cb, lab, dtb)
    start = jnp.zeros((HEADS, HEAD_DIM, STATE), jnp.float32)
    final, y_blocks = lax.scan(scan_step, start, (x_heads, b_all.reshape(blocks, BLOCK, STATE), c_all.reshape(blocks, BLOCK, STATE), log_decay.reshape(blocks, BLOCK, HEADS), step_dt.reshape(blocks, BLOCK, HEADS)))
    x_flat = x_conv.reshape(TOKENS, HEADS, HEAD_DIM)
    y_all = y_blocks.reshape(TOKENS, HEADS, HEAD_DIM) + skip_d[None, :, None] * x_flat
    mean_sq = lax.optimization_barrier(jnp.mean(y_all * y_all, axis=-1, keepdims=True))
    normed = (y_all * lax.rsqrt(mean_sq + 1e-05) * norm_gain.reshape(HEADS, HEAD_DIM)[None]).reshape(TOKENS, INNER).astype(jnp.bfloat16)
    return jnp.dot(normed, out_w, preferred_element_type=jnp.float32).astype(jnp.bfloat16)
```

```python
import functools

import jax
import jax.numpy as jnp
from jax import lax
from jax.experimental import pallas as pl
from jax.experimental.pallas import tpu as pltpu
from jax.sharding import PartitionSpec as P

MESH = pl.DeviceIdType.MESH
F32 = jnp.float32
BF16 = jnp.bfloat16
K_PARTS = 4
OUT_PARTS = 8
TILE = 256
LANES = 128


def dot(a, b):
    return jnp.dot(a, b, preferred_element_type=F32)


def split(v, parts):
    terms = []
    for _ in range(parts):
        term = v.astype(BF16)
        terms.append(term)
        v = v - term.astype(F32)
    return terms


def layer_kernel(
    ctx_size,
    tokens,
    in_x,
    in_bc,
    in_dt,
    out_w,
    conv_x,
    conv_bc,
    dt_bias,
    a_log,
    skip_d,
    gain,
    out,
    gath,
    w_in,
    w_dt,
    w_out,
    acc,
    acc_dt,
    ext,
    taps,
    xc,
    xdt,
    xtail,
    ecs,
    yb,
    score,
    end,
    st_in,
    st_out,
    normed,
    part,
    own,
    send1,
    recv1,
    send2,
    recv2,
    load_sem,
    tok_sem,
    a_send,
    a_recv,
    b_send,
    b_recv,
    f_send,
    f_recv,
    conv_sem,
    s_send,
    s_recv,
    r1_send,
    r1_recv,
    r2_send,
    r2_recv,
):
    c = lax.axis_index("ctx")
    t = lax.axis_index("tp")
    mate = t + 1 - 2 * (t % 2)
    across = (t + 2) % 4
    far = (mate + 2) % 4
    rows, depth = tokens.shape
    span = 4 * rows
    inner = in_x.shape[1]
    bc = in_bc.shape[1]
    wide = inner + bc
    states = bc // 2
    heads = dt_bias.shape[1]
    kc = depth // K_PARTS
    oc = depth // OUT_PARTS
    has_prev = c > 0
    has_next = c < ctx_size - 1

    def cols(i, size):
        return pl.ds(pl.multiple_of(i * size, size), size)

    def load(k):
        ks = cols(k, kc)
        return (
            pltpu.make_async_copy(in_x.at[ks, :], w_in.at[ks, 0:inner], load_sem.at[0, k]),
            pltpu.make_async_copy(in_bc.at[ks, :], w_in.at[ks, inner:wide], load_sem.at[1, k]),
        )

    load_dt = pltpu.make_async_copy(in_dt, w_dt, load_sem.at[2, 0])
    load_out = pltpu.make_async_copy(out_w, w_out, load_sem.at[2, 1])
    load_tok = pltpu.make_async_copy(tokens, gath.at[t], tok_sem)

    def remote(src, dst, send, recv, cc, tt):
        return pltpu.make_async_remote_copy(
            src_ref=src,
            dst_ref=dst,
            send_sem=send,
            recv_sem=recv,
            device_id=(cc, tt),
            device_id_type=MESH,
        )

    def copy_a(k):
        ks = cols(k, kc)
        return remote(
            tokens.at[:, ks], gath.at[t, :, ks], a_send.at[k], a_recv.at[k], c, across
        )

    def copy_b(k):
        ks = cols(k, kc)
        return remote(tokens.at[:, ks], gath.at[t, :, ks], b_send.at[k], b_recv.at[k], c, mate)

    def copy_f(k):
        ks = cols(k, kc)
        return remote(
            gath.at[across, :, ks], gath.at[across, :, ks], f_send.at[k], f_recv.at[k], c, mate
        )

    def got(block, k, send, recv):
        ks = cols(k, kc)
        return remote(
            gath.at[block, :, ks], gath.at[block, :, ks], send.at[k], recv.at[k], c, mate
        )

    barrier = pltpu.get_barrier_semaphore()
    for tt in (mate, across):
        pl.semaphore_signal(barrier, inc=1, device_id=(c, tt), device_id_type=MESH)

    @pl.when(has_prev)
    def _():
        pl.semaphore_signal(barrier, inc=1, device_id=(c - 1, t), device_id_type=MESH)

    @pl.when(has_next)
    def _():
        pl.semaphore_signal(barrier, inc=1, device_id=(c + 1, t), device_id_type=MESH)

    load_tok.start()
    load_dt.start()
    for k in range(K_PARTS):
        for copy in load(k):
            copy.start()
    load_out.start()

    peers = 2 + jnp.where(has_prev, 1, 0) + jnp.where(has_next, 1, 0)
    pl.semaphore_wait(barrier, peers)

    for k in range(K_PARTS):
        copy_a(k).start()
    for k in range(K_PARTS):
        copy_b(k).start()

    taps[:, 0:inner] = conv_x[...]
    taps[:, inner:wide] = conv_bc[...]
    acc[...] = jnp.zeros_like(acc)
    acc_dt[...] = jnp.zeros_like(acc_dt)

    @pl.when(c == 0)
    def _():
        ext[0:8, :] = jnp.zeros((8, wide), F32)
        st_in[...] = jnp.zeros_like(st_in)

    load_tok.wait()
    load_dt.wait()

    def project(k, _):
        ks = cols(k, kc)
        got(across, k, a_send, a_recv).wait_recv()
        copy_f(k).start()
        got(mate, k, b_send, b_recv).wait_recv()
        for copy in load(k):
            copy.wait()
        got(far, k, f_send, f_recv).wait_recv()
        lhs = gath[:, :, ks].reshape(span, kc)
        acc_dt[...] += dot(lhs, w_dt[ks, :])

        def tile(n, _):
            ns = cols(n, TILE)
            acc[:, ns] += dot(gath[:, :, ks].reshape(span, kc), w_in[ks, ns])
            return 0

        lax.fori_loop(0, wide // TILE, tile, 0)
        return 0

    lax.fori_loop(0, K_PARTS, project, 0)

    for n in range(wide // TILE):
        ns = slice(n * TILE, (n + 1) * TILE)
        ext[8 : 8 + span, ns] = acc[:, ns].astype(BF16).astype(F32)

    conv_send = remote(
        ext.at[span : span + 8, :], ext.at[0:8, :], conv_sem.at[0], conv_sem.at[1], c + 1, t
    )
    conv_recv = remote(
        ext.at[span : span + 8, :], ext.at[0:8, :], conv_sem.at[0], conv_sem.at[1], c - 1, t
    )

    @pl.when(has_next)
    def _():
        conv_send.start()

    dt = jax.nn.softplus(acc_dt[...] + dt_bias[...])
    la = -jnp.exp(a_log[...]) * dt
    later = lax.broadcasted_iota(jnp.int32, (span, span), 0)
    earlier = lax.broadcasted_iota(jnp.int32, (span, span), 1)
    tri = later >= earlier
    tri_b = jnp.where(tri, 1.0, 0.0).astype(BF16)
    cs = sum(dot(tri_b, term) for term in split(la, 3))
    cs_t = cs.T
    last = cs[span - 1 : span, :]
    head_width = inner // heads
    head_of = lax.broadcasted_iota(jnp.int32, (heads, inner), 1) // head_width
    head_at = lax.broadcasted_iota(jnp.int32, (heads, inner), 0)
    spread = jnp.where(head_of == head_at, 1.0, 0.0).astype(BF16)

    def expand(v):
        hi, lo = split(v, 2)
        return dot(hi, spread) + dot(lo, spread)

    ecs[...] = expand(jnp.exp(cs))
    skip = expand(jnp.broadcast_to(skip_d[...], (8, heads)))[0:1, :]
    dt_wide = expand(dt)
    dtail_wide = expand(dt * jnp.exp(last - cs))

    @pl.when(has_prev)
    def _():
        conv_recv.wait_recv()

    for n in range(wide // TILE):
        ns = slice(n * TILE, (n + 1) * TILE)
        total = taps[0:1, ns] * ext[5 : 5 + span, ns]
        for k in range(1, 4):
            total = total + taps[k : k + 1, ns] * ext[5 + k : 5 + k + span, ns]
        x = total / (1.0 + jnp.exp(-total))
        xc[:, ns] = x
        if n * TILE < inner:
            xdt[:, ns] = (x * dt_wide[:, ns]).astype(BF16)
            xtail[:, ns] = (x * dtail_wide[:, ns]).astype(BF16)

    b_t = xc[:, inner : inner + states].T.astype(BF16)
    c_b = xc[:, inner + states : wide].astype(BF16)
    end[...] = dot(b_t, xtail[...])

    parts = inner // LANES

    def state_send(j):
        return remote(st_out.at[j], st_in.at[j], s_send.at[j], s_recv.at[j], c + 1, t)

    def state_recv(j):
        return remote(st_out.at[j], st_in.at[j], s_send.at[j], s_recv.at[j], c - 1, t)

    def relay():
        for j in range(parts):
            ls = slice(j * LANES, (j + 1) * LANES)

            @pl.when(has_prev)
            def _():
                state_recv(j).wait_recv()

            @pl.when(has_next)
            def _():
                decay = ecs[span - 1 : span, ls]
                st_out[j] = (decay * st_in[j].astype(F32) + end[:, ls]).astype(BF16)
                state_send(j).start()

    @pl.when(c < 2)
    def _():
        relay()

    score[...] = jnp.where(tri, dot(c_b, b_t), 0.0)
    low_head = lax.broadcasted_iota(jnp.int32, (LANES, LANES), 1) < head_width
    for j in range(parts):
        ls = slice(j * LANES, (j + 1) * LANES)
        for r in range(span // LANES):
            rs = slice(r * LANES, (r + 1) * LANES)
            upto = (r + 1) * LANES
            both = []
            for h in (2 * j, 2 * j + 1):
                diff = cs[rs, h : h + 1] - cs_t[h : h + 1, 0:upto]
                weights = score[rs, 0:upto] * jnp.exp(jnp.minimum(diff, 0.0))
                both.append(dot(weights.astype(BF16), xdt[0:upto, ls]))
            yb[rs, ls] = jnp.where(low_head, both[0], both[1]) + skip[:, ls] * xc[rs, ls]

    @pl.when(c >= 2)
    def _():
        relay()

    same = (
        lax.broadcasted_iota(jnp.int32, (2 * LANES, LANES), 0) % LANES // head_width
        == lax.broadcasted_iota(jnp.int32, (2 * LANES, LANES), 1) // head_width
    )
    same = jnp.where(same, 1.0 / head_width, 0.0).astype(BF16)
    for j in range(parts):
        ls = slice(j * LANES, (j + 1) * LANES)
        y = yb[:, ls] + ecs[:, ls] * dot(c_b, st_in[j])
        mean_sq = dot(jnp.concatenate(split(y * y, 2), axis=1), same)
        normed[:, ls] = (y * lax.rsqrt(mean_sq + 1e-5) * gain[:, ls]).astype(BF16)

    load_out.wait()

    def hop1(j):
        return remote(send1.at[j], recv1.at[j], r1_send.at[j], r1_recv.at[j], c, mate)

    def hop2(j):
        return remote(send2.at[j], recv2.at[j], r2_send.at[j], r2_recv.at[j], c, across)

    def multiply(j):
        prod = dot(normed[...], w_out[:, cols(j, oc)])
        part[...] = prod.reshape(4, rows, oc)
        send1[j, 0] = part[far].astype(BF16)
        send1[j, 1] = part[mate].astype(BF16)
        hop1(j).start()
        own[j, 0] = part[across]
        own[j, 1] = part[t]

    def pass_on(j):
        hop1(j).wait_recv()
        send2[j] = (own[j, 0] + recv1[j, 0].astype(F32)).astype(BF16)
        hop2(j).start()

    multiply(0)

    def step(j, _):
        multiply(j)
        pass_on(j - 1)
        return 0

    lax.fori_loop(1, OUT_PARTS, step, 0)
    pass_on(OUT_PARTS - 1)

    def finish(j, _):
        hop2(j).wait_recv()
        total = own[j, 1] + recv1[j, 1].astype(F32) + recv2[j].astype(F32)
        out[:, cols(j, oc)] = total.astype(BF16)
        return 0

    lax.fori_loop(0, OUT_PARTS, finish, 0)

    def drain_k(k, _):
        copy_a(k).wait_send()
        copy_b(k).wait_send()
        copy_f(k).wait_send()
        return 0

    lax.fori_loop(0, K_PARTS, drain_k, 0)

    def drain_o(j, _):
        hop1(j).wait_send()
        hop2(j).wait_send()
        return 0

    lax.fori_loop(0, OUT_PARTS, drain_o, 0)

    @pl.when(has_next)
    def _():
        conv_send.wait_send()
        for j in range(parts):
            state_send(j).wait_send()


def per_device(
    ctx_size, tokens, in_x, in_bc, in_dt, conv_x, conv_bc, dt_bias, a_log, skip_d, norm_gain, out_w
):
    rows, depth = tokens.shape
    span = 4 * rows
    inner = in_x.shape[1]
    wide = inner + in_bc.shape[1]
    states = in_bc.shape[1] // 2
    heads = a_log.shape[0]
    parts = inner // LANES
    oc = depth // OUT_PARTS
    dma = pltpu.SemaphoreType.DMA
    anywhere = pl.BlockSpec(memory_space=pl.ANY)
    local = pl.BlockSpec(memory_space=pltpu.VMEM)
    return pl.pallas_call(
        functools.partial(layer_kernel, ctx_size),
        out_shape=jax.ShapeDtypeStruct((rows, depth), BF16),
        in_specs=[anywhere] * 5 + [local] * 6,
        out_specs=local,
        scratch_shapes=[
            pltpu.VMEM((4, rows, depth), BF16),
            pltpu.VMEM((depth, wide), BF16),
            pltpu.VMEM((depth, heads), BF16),
            pltpu.VMEM((inner, depth), BF16),
            pltpu.VMEM((span, wide), F32),
            pltpu.VMEM((span, heads), F32),
            pltpu.VMEM((span + 8, wide), F32),
            pltpu.VMEM((4, wide), F32),
            pltpu.VMEM((span, wide), F32),
            pltpu.VMEM((span, inner), BF16),
            pltpu.VMEM((span, inner), BF16),
            pltpu.VMEM((span, inner), F32),
            pltpu.VMEM((span, inner), F32),
            pltpu.VMEM((span, span), F32),
            pltpu.VMEM((states, inner), F32),
            pltpu.VMEM((parts, states, LANES), BF16),
            pltpu.VMEM((parts, states, LANES), BF16),
            pltpu.VMEM((span, inner), BF16),
            pltpu.VMEM((4, rows, oc), F32),
            pltpu.VMEM((OUT_PARTS, 2, rows, oc), F32),
            pltpu.VMEM((OUT_PARTS, 2, rows, oc), BF16),
            pltpu.VMEM((OUT_PARTS, 2, rows, oc), BF16),
            pltpu.VMEM((OUT_PARTS, rows, oc), BF16),
            pltpu.VMEM((OUT_PARTS, rows, oc), BF16),
            dma((3, K_PARTS)),
            dma(()),
            dma((K_PARTS,)),
            dma((K_PARTS,)),
            dma((K_PARTS,)),
            dma((K_PARTS,)),
            dma((K_PARTS,)),
            dma((K_PARTS,)),
            dma((2,)),
            dma((parts,)),
            dma((parts,)),
            dma((OUT_PARTS,)),
            dma((OUT_PARTS,)),
            dma((OUT_PARTS,)),
            dma((OUT_PARTS,)),
        ],
        compiler_params=pltpu.CompilerParams(
            collective_id=0, has_side_effects=True, vmem_limit_bytes=56 * 2**20
        ),
    )(
        tokens,
        in_x,
        in_bc,
        in_dt,
        out_w,
        conv_x,
        conv_bc,
        dt_bias.reshape(1, heads),
        a_log.reshape(1, heads),
        skip_d.reshape(1, heads),
        norm_gain.reshape(1, inner),
    )


def solution(mesh):
    return jax.shard_map(
        functools.partial(per_device, mesh.shape["ctx"]),
        mesh=mesh,
        in_specs=(
            P(("ctx", "tp"), None),
            P(None, "tp"),
            P(),
            P(None, "tp"),
            P(None, "tp"),
            P(),
            P("tp"),
            P("tp"),
            P("tp"),
            P("tp"),
            P("tp", None),
        ),
        out_specs=P(("ctx", "tp"), None),
        check_vma=False,
    )
```

```python
import functools

import jax
import jax.numpy as jnp
from jax import lax
from jax.experimental import pallas as pl
from jax.experimental.pallas import tpu as pltpu
from jax.sharding import PartitionSpec as P

MESH = pl.DeviceIdType.MESH
F32 = jnp.float32
BF16 = jnp.bfloat16
K_PARTS = 8
OUT_PARTS = 8
TILE = 256
LANES = 128


def dot(a, b):
    return jnp.dot(a, b, preferred_element_type=F32)


def split(v, parts):
    terms = []
    for _ in range(parts):
        term = v.astype(BF16)
        terms.append(term)
        v = v - term.astype(F32)
    return terms


def layer_kernel(
    ctx_size,
    tokens,
    in_x,
    in_bc,
    in_dt,
    out_w,
    conv_x,
    conv_bc,
    dt_bias,
    a_log,
    skip_d,
    gain,
    out,
    gath,
    w_in,
    w_dt,
    w_out,
    acc,
    acc_dt,
    ext,
    taps,
    xc,
    xdt,
    xtail,
    ecs,
    yb,
    score,
    end,
    st_in,
    x_out,
    x_in,
    g_out,
    g_in,
    p_out,
    pair_decay,
    normed,
    part,
    own,
    send1,
    recv1,
    send2,
    recv2,
    load_sem,
    tok_sem,
    a_send,
    a_recv,
    b_send,
    b_recv,
    f_send,
    f_recv,
    conv_sem,
    d_sem,
    x_send,
    x_recv,
    g_send,
    g_recv,
    p_send,
    p_recv,
    r1_send,
    r1_recv,
    r2_send,
    r2_recv,
):
    c = lax.axis_index("ctx")
    t = lax.axis_index("tp")
    mate = t + 1 - 2 * (t % 2)
    across = (t + 2) % 4
    far = (mate + 2) % 4
    rows, depth = tokens.shape
    span = 4 * rows
    inner = in_x.shape[1]
    bc = in_bc.shape[1]
    wide = inner + bc
    states = bc // 2
    heads = dt_bias.shape[1]
    kc = depth // K_PARTS
    oc = depth // OUT_PARTS
    has_prev = c > 0
    has_next = c < ctx_size - 1
    has_prev2 = c > 1
    has_next2 = c < ctx_size - 2
    odd = c % 2
    pair = c + 1 - 2 * odd
    parts = inner // LANES
    half = parts // 2

    def cols(i, size):
        return pl.ds(pl.multiple_of(i * size, size), size)

    def load(k):
        ks = cols(k, kc)
        return (
            pltpu.make_async_copy(in_x.at[ks, :], w_in.at[ks, 0:inner], load_sem.at[0, k]),
            pltpu.make_async_copy(in_bc.at[ks, :], w_in.at[ks, inner:wide], load_sem.at[1, k]),
        )

    load_dt = pltpu.make_async_copy(in_dt, w_dt, load_sem.at[2, 0])
    load_out = pltpu.make_async_copy(out_w, w_out, load_sem.at[2, 1])
    load_tok = pltpu.make_async_copy(tokens, gath.at[t], tok_sem)

    def remote(src, dst, send, recv, cc, tt):
        return pltpu.make_async_remote_copy(
            src_ref=src,
            dst_ref=dst,
            send_sem=send,
            recv_sem=recv,
            device_id=(cc, tt),
            device_id_type=MESH,
        )

    def copy_a(k):
        ks = cols(k, kc)
        return remote(
            tokens.at[:, ks], gath.at[t, :, ks], a_send.at[k], a_recv.at[k], c, across
        )

    def copy_b(k):
        ks = cols(k, kc)
        return remote(tokens.at[:, ks], gath.at[t, :, ks], b_send.at[k], b_recv.at[k], c, mate)

    def copy_f(k):
        ks = cols(k, kc)
        return remote(
            gath.at[across, :, ks], gath.at[across, :, ks], f_send.at[k], f_recv.at[k], c, mate
        )

    def got(block, k, send, recv):
        ks = cols(k, kc)
        return remote(
            gath.at[block, :, ks], gath.at[block, :, ks], send.at[k], recv.at[k], c, mate
        )

    barrier = pltpu.get_barrier_semaphore()
    for tt in (mate, across):
        pl.semaphore_signal(barrier, inc=1, device_id=(c, tt), device_id_type=MESH)

    @pl.when(has_prev)
    def _():
        pl.semaphore_signal(barrier, inc=1, device_id=(c - 1, t), device_id_type=MESH)

    @pl.when(has_next)
    def _():
        pl.semaphore_signal(barrier, inc=1, device_id=(c + 1, t), device_id_type=MESH)

    @pl.when(has_prev2)
    def _():
        pl.semaphore_signal(barrier, inc=1, device_id=(c - 2, t), device_id_type=MESH)

    @pl.when(has_next2)
    def _():
        pl.semaphore_signal(barrier, inc=1, device_id=(c + 2, t), device_id_type=MESH)

    load_tok.start()
    load_dt.start()
    for k in range(K_PARTS):
        for copy in load(k):
            copy.start()
    load_out.start()

    peers = 2
    for flag in (has_prev, has_next, has_prev2, has_next2):
        peers = peers + jnp.where(flag, 1, 0)
    pl.semaphore_wait(barrier, peers)

    for k in range(K_PARTS):
        copy_a(k).start()
    for k in range(K_PARTS):
        copy_b(k).start()

    taps[:, 0:inner] = conv_x[...]
    taps[:, inner:wide] = conv_bc[...]
    acc[...] = jnp.zeros_like(acc)
    acc_dt[...] = jnp.zeros_like(acc_dt)

    @pl.when(c == 0)
    def _():
        ext[0:8, :] = jnp.zeros((8, wide), F32)

    @pl.when(c < 2)
    def _():
        g_in[...] = jnp.zeros_like(g_in)

    load_tok.wait()
    load_dt.wait()

    def project(k, _):
        ks = cols(k, kc)
        got(across, k, a_send, a_recv).wait_recv()
        copy_f(k).start()
        got(mate, k, b_send, b_recv).wait_recv()
        for copy in load(k):
            copy.wait()
        got(far, k, f_send, f_recv).wait_recv()
        lhs = gath[:, :, ks].reshape(span, kc)
        acc_dt[...] += lax.dot_general(
            lhs, w_dt[:, ks], (((1,), (1,)), ((), ())), preferred_element_type=F32
        )

        def tile(n, _):
            ns = cols(n, TILE)
            acc[:, ns] += dot(gath[:, :, ks].reshape(span, kc), w_in[ks, ns])
            return 0

        lax.fori_loop(0, wide // TILE, tile, 0)
        return 0

    lax.fori_loop(0, K_PARTS, project, 0)

    ext[span : span + 8, :] = acc[span - 8 : span, :].astype(BF16).astype(F32)
    conv_send = remote(
        ext.at[span : span + 8, :], ext.at[0:8, :], conv_sem.at[0], conv_sem.at[1], c + 1, t
    )
    conv_recv = remote(
        ext.at[span : span + 8, :], ext.at[0:8, :], conv_sem.at[0], conv_sem.at[1], c - 1, t
    )

    @pl.when(has_next)
    def _():
        conv_send.start()

    for n in range(wide // TILE):
        ns = slice(n * TILE, (n + 1) * TILE)
        ext[8:span, ns] = acc[0 : span - 8, ns].astype(BF16).astype(F32)

    dt = jax.nn.softplus(acc_dt[...] + dt_bias[...])
    la = -jnp.exp(a_log[...]) * dt
    later = lax.broadcasted_iota(jnp.int32, (span, span), 0)
    earlier = lax.broadcasted_iota(jnp.int32, (span, span), 1)
    tri = later >= earlier
    tri_b = jnp.where(tri, 1.0, 0.0).astype(BF16)
    cs = sum(dot(tri_b, term) for term in split(la, 3))
    cs_t = cs.T
    last = cs[span - 1 : span, :]
    head_width = inner // heads
    head_of = lax.broadcasted_iota(jnp.int32, (heads, inner), 1) // head_width
    head_at = lax.broadcasted_iota(jnp.int32, (heads, inner), 0)
    spread = jnp.where(head_of == head_at, 1.0, 0.0).astype(BF16)

    def expand(v):
        hi, lo = split(v, 2)
        return dot(hi, spread) + dot(lo, spread)

    ecs[...] = expand(jnp.exp(cs))

    theirs = cols(1 - odd, inner // 2)
    decay_swap = remote(
        ecs.at[span - 8 : span, theirs], pair_decay, d_sem.at[0], d_sem.at[1], pair, t
    )
    decay_swap.start()
    skip = expand(jnp.broadcast_to(skip_d[...], (8, heads)))[0:1, :]
    dt_wide = expand(dt)
    dtail_wide = expand(dt * jnp.exp(last - cs))

    @pl.when(has_prev)
    def _():
        conv_recv.wait_recv()

    for n in range(wide // TILE):
        ns = slice(n * TILE, (n + 1) * TILE)
        total = taps[0:1, ns] * ext[5 : 5 + span, ns]
        for k in range(1, 4):
            total = total + taps[k : k + 1, ns] * ext[5 + k : 5 + k + span, ns]
        x = total / (1.0 + jnp.exp(-total))
        xc[:, ns] = x
        if n * TILE < inner:
            xdt[:, ns] = (x * dt_wide[:, ns]).astype(BF16)
            xtail[:, ns] = (x * dtail_wide[:, ns]).astype(BF16)

    b_t = xc[:, inner : inner + states].T.astype(BF16)
    c_b = xc[:, inner + states : wide].astype(BF16)

    def end_swap(i):
        return remote(x_out.at[i], x_in.at[i], x_send.at[i], x_recv.at[i], pair, t)

    def hand_down(i, cc):
        return remote(g_out.at[i], g_in.at[i], g_send.at[i], g_recv.at[i], cc, t)

    def share(i):
        j = odd * half + i
        return remote(p_out.at[i], st_in.at[j], p_send.at[i], p_recv.at[i], pair, t)

    def shared(i):
        j = (1 - odd) * half + i
        return remote(p_out.at[i], st_in.at[j], p_send.at[i], p_recv.at[i], pair, t)

    def ends(i, _):
        j = (1 - odd) * half + i
        x_out[i] = dot(b_t, xtail[:, cols(j, LANES)]).astype(BF16)
        end_swap(i).start()
        return 0

    def own_ends(i, _):
        j = odd * half + i
        end[i] = dot(b_t, xtail[:, cols(j, LANES)])
        return 0

    lax.fori_loop(0, half, ends, 0)
    lax.fori_loop(0, half, own_ends, 0)
    decay_swap.wait_recv()

    def relay():
        def part_of(i, _):
            ls = cols(i, LANES)
            mine = ecs[span - 8 : span, cols(odd * half + i, LANES)][7:8, :]
            other = pair_decay[:, ls][7:8, :]
            end_swap(i).wait_recv()
            end_mine = end[i]
            end_other = x_in[i].astype(F32)

            @pl.when(has_prev2)
            def _():
                hand_down(i, c - 2).wait_recv()

            even = odd == 0
            first = g_in[i].astype(F32)
            second = jnp.where(even, mine, other) * first + jnp.where(even, end_mine, end_other)

            @pl.when(has_next2)
            def _():
                after = jnp.where(even, other, mine) * second
                after = after + jnp.where(even, end_other, end_mine)
                g_out[i] = after.astype(BF16)
                hand_down(i, c + 2).start()

            p_out[i] = jnp.where(even, second, first).astype(BF16)
            share(i).start()
            st_in[odd * half + i] = jnp.where(even, first, second).astype(BF16)
            return 0

        lax.fori_loop(0, half, part_of, 0)

    @pl.when(c < 2)
    def _():
        relay()

    score[...] = jnp.where(tri, dot(c_b, b_t), 0.0)
    low_head = lax.broadcasted_iota(jnp.int32, (LANES, LANES), 1) < head_width
    for j in range(parts):
        if j == parts // 2:

            @pl.when((c >= 2) & (c < 4))
            def _():
                relay()

        ls = slice(j * LANES, (j + 1) * LANES)
        for r in range(span // LANES):
            rs = slice(r * LANES, (r + 1) * LANES)
            upto = (r + 1) * LANES
            both = []
            for h in (2 * j, 2 * j + 1):
                diff = cs[rs, h : h + 1] - cs_t[h : h + 1, 0:upto]
                weights = score[rs, 0:upto] * jnp.exp(jnp.minimum(diff, 0.0))
                both.append(dot(weights.astype(BF16), xdt[0:upto, ls]))
            yb[rs, ls] = jnp.where(low_head, both[0], both[1]) + skip[:, ls] * xc[rs, ls]

    @pl.when(c >= 4)
    def _():
        relay()

    same = (
        lax.broadcasted_iota(jnp.int32, (2 * LANES, LANES), 0) % LANES // head_width
        == lax.broadcasted_iota(jnp.int32, (2 * LANES, LANES), 1) // head_width
    )
    same = jnp.where(same, 1.0 / head_width, 0.0).astype(BF16)
    for i in range(half):
        shared(i).wait_recv()
    for j in range(parts):
        ls = slice(j * LANES, (j + 1) * LANES)
        y = yb[:, ls] + ecs[:, ls] * dot(c_b, st_in[j])
        mean_sq = dot(jnp.concatenate(split(y * y, 2), axis=1), same)
        normed[:, ls] = (y * lax.rsqrt(mean_sq + 1e-5) * gain[:, ls]).astype(BF16)

    load_out.wait()

    def hop1(j):
        return remote(send1.at[j], recv1.at[j], r1_send.at[j], r1_recv.at[j], c, mate)

    def hop2(j):
        return remote(send2.at[j], recv2.at[j], r2_send.at[j], r2_recv.at[j], c, across)

    def multiply(j):
        prod = dot(normed[...], w_out[:, cols(j, oc)])
        part[...] = prod.reshape(4, rows, oc)
        send1[j, 0] = part[far].astype(BF16)
        send1[j, 1] = part[mate].astype(BF16)
        hop1(j).start()
        own[j, 0] = part[across]
        own[j, 1] = part[t]

    def pass_on(j):
        hop1(j).wait_recv()
        send2[j] = (own[j, 0] + recv1[j, 0].astype(F32)).astype(BF16)
        hop2(j).start()

    multiply(0)

    def step(j, _):
        multiply(j)
        pass_on(j - 1)
        return 0

    lax.fori_loop(1, OUT_PARTS, step, 0)
    pass_on(OUT_PARTS - 1)

    def finish(j, _):
        hop2(j).wait_recv()
        total = own[j, 1] + recv1[j, 1].astype(F32) + recv2[j].astype(F32)
        out[:, cols(j, oc)] = total
        return 0

    lax.fori_loop(0, OUT_PARTS, finish, 0)

    def drain_k(k, _):
        copy_a(k).wait_send()
        copy_b(k).wait_send()
        copy_f(k).wait_send()
        return 0

    lax.fori_loop(0, K_PARTS, drain_k, 0)

    def drain_o(j, _):
        hop1(j).wait_send()
        hop2(j).wait_send()
        return 0

    lax.fori_loop(0, OUT_PARTS, drain_o, 0)

    decay_swap.wait_send()

    def drain_s(i, _):
        end_swap(i).wait_send()
        share(i).wait_send()
        return 0

    lax.fori_loop(0, half, drain_s, 0)

    @pl.when(has_next)
    def _():
        conv_send.wait_send()

    @pl.when(has_next2)
    def _():
        def drain_g(i, _):
            hand_down(i, c + 2).wait_send()
            return 0

        lax.fori_loop(0, half, drain_g, 0)


def per_device(
    ctx_size, tokens, in_x, in_bc, in_dt, conv_x, conv_bc, dt_bias, a_log, skip_d, norm_gain, out_w
):
    rows, depth = tokens.shape
    span = 4 * rows
    inner = in_x.shape[1]
    wide = inner + in_bc.shape[1]
    states = in_bc.shape[1] // 2
    heads = a_log.shape[0]
    parts = inner // LANES
    half = parts // 2
    oc = depth // OUT_PARTS
    dma = pltpu.SemaphoreType.DMA
    anywhere = pl.BlockSpec(memory_space=pl.ANY)
    local = pl.BlockSpec(memory_space=pltpu.VMEM)
    total = pl.pallas_call(
        functools.partial(layer_kernel, ctx_size),
        out_shape=jax.ShapeDtypeStruct((rows, depth), F32),
        in_specs=[anywhere] * 5 + [local] * 6,
        out_specs=local,
        scratch_shapes=[
            pltpu.VMEM((4, rows, depth), BF16),
            pltpu.VMEM((depth, wide), BF16),
            pltpu.VMEM((heads, depth), BF16),
            pltpu.VMEM((inner, depth), BF16),
            pltpu.VMEM((span, wide), F32),
            pltpu.VMEM((span, heads), F32),
            pltpu.VMEM((span + 8, wide), F32),
            pltpu.VMEM((4, wide), F32),
            pltpu.VMEM((span, wide), F32),
            pltpu.VMEM((span, inner), BF16),
            pltpu.VMEM((span, inner), BF16),
            pltpu.VMEM((span, inner), F32),
            pltpu.VMEM((span, inner), F32),
            pltpu.VMEM((span, span), F32),
            pltpu.VMEM((half, states, LANES), F32),
            pltpu.VMEM((parts, states, LANES), BF16),
            pltpu.VMEM((half, states, LANES), BF16),
            pltpu.VMEM((half, states, LANES), BF16),
            pltpu.VMEM((half, states, LANES), BF16),
            pltpu.VMEM((half, states, LANES), BF16),
            pltpu.VMEM((half, states, LANES), BF16),
            pltpu.VMEM((8, inner // 2), F32),
            pltpu.VMEM((span, inner), BF16),
            pltpu.VMEM((4, rows, oc), F32),
            pltpu.VMEM((OUT_PARTS, 2, rows, oc), F32),
            pltpu.VMEM((OUT_PARTS, 2, rows, oc), BF16),
            pltpu.VMEM((OUT_PARTS, 2, rows, oc), BF16),
            pltpu.VMEM((OUT_PARTS, rows, oc), BF16),
            pltpu.VMEM((OUT_PARTS, rows, oc), BF16),
            dma((3, K_PARTS)),
            dma(()),
            dma((K_PARTS,)),
            dma((K_PARTS,)),
            dma((K_PARTS,)),
            dma((K_PARTS,)),
            dma((K_PARTS,)),
            dma((K_PARTS,)),
            dma((2,)),
            dma((2,)),
            dma((half,)),
            dma((half,)),
            dma((half,)),
            dma((half,)),
            dma((half,)),
            dma((half,)),
            dma((OUT_PARTS,)),
            dma((OUT_PARTS,)),
            dma((OUT_PARTS,)),
            dma((OUT_PARTS,)),
        ],
        compiler_params=pltpu.CompilerParams(
            collective_id=0, has_side_effects=True, vmem_limit_bytes=56 * 2**20
        ),
    )(
        tokens,
        in_x,
        in_bc,
        in_dt.T,
        out_w,
        conv_x,
        conv_bc,
        dt_bias.reshape(1, heads),
        a_log.reshape(1, heads),
        skip_d.reshape(1, heads),
        norm_gain.reshape(1, inner),
    )
    return total.astype(BF16)


def solution(mesh):
    return jax.shard_map(
        functools.partial(per_device, mesh.shape["ctx"]),
        mesh=mesh,
        in_specs=(
            P(("ctx", "tp"), None),
            P(None, "tp"),
            P(),
            P(None, "tp"),
            P(None, "tp"),
            P(),
            P("tp"),
            P("tp"),
            P("tp"),
            P("tp"),
            P("tp", None),
        ),
        out_specs=P(("ctx", "tp"), None),
        check_vma=False,
    )
```

```python
import functools

import jax
import jax.numpy as jnp
from jax import lax
from jax.experimental import pallas as pl
from jax.experimental.pallas import tpu as pltpu
from jax.sharding import PartitionSpec as P

MESH = pl.DeviceIdType.MESH
F32 = jnp.float32
BF16 = jnp.bfloat16
K_PARTS = 8
OUT_PARTS = 8
TILE = 256
LANES = 128


def dot(a, b):
    return jnp.dot(a, b, preferred_element_type=F32)


def split(v, parts):
    terms = []
    for _ in range(parts):
        term = v.astype(BF16)
        terms.append(term)
        v = v - term.astype(F32)
    return terms


def layer_kernel(
    ctx_size,
    tokens,
    in_x,
    in_bc,
    in_dt,
    out_w,
    conv_x,
    conv_bc,
    dt_bias,
    a_log,
    skip_d,
    gain,
    out,
    gath,
    w_in,
    w_dt,
    w_out,
    acc,
    acc_dt,
    ext,
    taps,
    xc,
    xdt,
    xtail,
    ecs,
    tri_t,
    spread,
    yb,
    score,
    end,
    st_in,
    x_out,
    x_in,
    g_out,
    g_in,
    p_out,
    pair_decay,
    normed,
    part,
    own,
    send1,
    recv1,
    send2,
    recv2,
    load_sem,
    tok_sem,
    a_send,
    a_recv,
    b_send,
    b_recv,
    f_send,
    f_recv,
    conv_sem,
    d_sem,
    x_send,
    x_recv,
    g_send,
    g_recv,
    p_send,
    p_recv,
    r1_send,
    r1_recv,
    r2_send,
    r2_recv,
):
    c = lax.axis_index("ctx")
    t = lax.axis_index("tp")
    mate = t + 1 - 2 * (t % 2)
    across = (t + 2) % 4
    far = (mate + 2) % 4
    rows, depth = tokens.shape
    span = 4 * rows
    inner = in_x.shape[1]
    bc = in_bc.shape[1]
    wide = inner + bc
    states = bc // 2
    heads = dt_bias.shape[1]
    kc = depth // K_PARTS
    oc = depth // OUT_PARTS
    has_prev = c > 0
    has_next = c < ctx_size - 1
    has_prev2 = c > 1
    has_next2 = c < ctx_size - 2
    odd = c % 2
    pair = c + 1 - 2 * odd
    parts = inner // LANES
    half = parts // 2

    def cols(i, size):
        return pl.ds(pl.multiple_of(i * size, size), size)

    def load(k):
        ks = cols(k, kc)
        return (
            pltpu.make_async_copy(in_x.at[ks, :], w_in.at[ks, 0:inner], load_sem.at[0, k]),
            pltpu.make_async_copy(in_bc.at[ks, :], w_in.at[ks, inner:wide], load_sem.at[1, k]),
        )

    load_dt = pltpu.make_async_copy(in_dt, w_dt, load_sem.at[2, 0])
    load_out = pltpu.make_async_copy(out_w, w_out, load_sem.at[2, 1])
    load_tok = pltpu.make_async_copy(tokens, gath.at[t], tok_sem)

    def remote(src, dst, send, recv, cc, tt):
        return pltpu.make_async_remote_copy(
            src_ref=src,
            dst_ref=dst,
            send_sem=send,
            recv_sem=recv,
            device_id=(cc, tt),
            device_id_type=MESH,
        )

    def copy_a(k):
        ks = cols(k, kc)
        return remote(
            tokens.at[:, ks], gath.at[t, :, ks], a_send.at[k], a_recv.at[k], c, across
        )

    def copy_b(k):
        ks = cols(k, kc)
        return remote(tokens.at[:, ks], gath.at[t, :, ks], b_send.at[k], b_recv.at[k], c, mate)

    def copy_f(k):
        ks = cols(k, kc)
        return remote(
            gath.at[across, :, ks], gath.at[across, :, ks], f_send.at[k], f_recv.at[k], c, mate
        )

    def got(block, k, send, recv):
        ks = cols(k, kc)
        return remote(
            gath.at[block, :, ks], gath.at[block, :, ks], send.at[k], recv.at[k], c, mate
        )

    barrier = pltpu.get_barrier_semaphore()
    for tt in (mate, across):
        pl.semaphore_signal(barrier, inc=1, device_id=(c, tt), device_id_type=MESH)

    @pl.when(has_prev)
    def _():
        pl.semaphore_signal(barrier, inc=1, device_id=(c - 1, t), device_id_type=MESH)

    @pl.when(has_next)
    def _():
        pl.semaphore_signal(barrier, inc=1, device_id=(c + 1, t), device_id_type=MESH)

    @pl.when(has_prev2)
    def _():
        pl.semaphore_signal(barrier, inc=1, device_id=(c - 2, t), device_id_type=MESH)

    @pl.when(has_next2)
    def _():
        pl.semaphore_signal(barrier, inc=1, device_id=(c + 2, t), device_id_type=MESH)

    load_tok.start()
    load_dt.start()
    for k in range(K_PARTS):
        for copy in load(k):
            copy.start()
    load_out.start()

    peers = 2
    for flag in (has_prev, has_next, has_prev2, has_next2):
        peers = peers + jnp.where(flag, 1, 0)
    pl.semaphore_wait(barrier, peers)

    for k in range(K_PARTS):
        copy_a(k).start()
    for k in range(K_PARTS):
        copy_b(k).start()

    taps[:, 0:inner] = conv_x[...]
    taps[:, inner:wide] = conv_bc[...]
    acc[...] = jnp.zeros_like(acc)
    acc_dt[...] = jnp.zeros_like(acc_dt)

    @pl.when(c == 0)
    def _():
        ext[0:8, :] = jnp.zeros((8, wide), F32)

    @pl.when(c < 2)
    def _():
        g_in[...] = jnp.zeros_like(g_in)

    head_width = inner // heads
    fields = 8 * heads
    earlier = lax.broadcasted_iota(jnp.int32, (span, span), 0)
    later = lax.broadcasted_iota(jnp.int32, (span, span), 1)
    tri_t[...] = jnp.where(later >= earlier, 1.0, 0.0).astype(BF16)
    field = lax.broadcasted_iota(jnp.int32, (fields, 3 * LANES), 0)
    lane = lax.broadcasted_iota(jnp.int32, (fields, 3 * LANES), 1)
    for j in range(parts):
        head = (lane % LANES + j * LANES) // head_width
        hit = (field % heads == head) & (field // (2 * heads) == lane // LANES)
        spread[j] = jnp.where(hit, 1.0, 0.0).astype(BF16)
    eye = lax.broadcasted_iota(jnp.int32, (heads, heads), 0) == lax.broadcasted_iota(
        jnp.int32, (heads, heads), 1
    )

    def upright(row):
        return jnp.sum(jnp.where(eye, row, 0.0), axis=1, keepdims=True)

    bias = upright(dt_bias[...])
    rate = -jnp.exp(upright(a_log[...]))
    skip_col = jnp.broadcast_to(upright(skip_d[...]), (heads, LANES))

    load_tok.wait()
    load_dt.wait()

    def project(k, _):
        ks = cols(k, kc)
        got(across, k, a_send, a_recv).wait_recv()
        copy_f(k).start()
        got(mate, k, b_send, b_recv).wait_recv()
        for copy in load(k):
            copy.wait()
        got(far, k, f_send, f_recv).wait_recv()
        lhs = gath[:, :, ks].reshape(span, kc)
        acc_dt[...] += lax.dot_general(
            w_dt[:, ks], lhs, (((1,), (1,)), ((), ())), preferred_element_type=F32
        )

        for n in range(wide // TILE):
            ns = slice(n * TILE, (n + 1) * TILE)
            acc[:, ns] += dot(lhs, w_in[ks, ns])
        return 0

    lax.fori_loop(0, K_PARTS, project, 0)

    ext[span : span + 8, :] = acc[span - 8 : span, :].astype(BF16).astype(F32)
    conv_send = remote(
        ext.at[span : span + 8, :], ext.at[0:8, :], conv_sem.at[0], conv_sem.at[1], c + 1, t
    )
    conv_recv = remote(
        ext.at[span : span + 8, :], ext.at[0:8, :], conv_sem.at[0], conv_sem.at[1], c - 1, t
    )

    @pl.when(has_next)
    def _():
        conv_send.start()

    for n in range(wide // TILE):
        ns = slice(n * TILE, (n + 1) * TILE)
        ext[8:span, ns] = acc[0 : span - 8, ns].astype(BF16).astype(F32)

    v = acc_dt[...] + bias
    dt = jnp.maximum(v, 0.0) + jnp.log1p(jnp.exp(-jnp.abs(v)))
    sums = dot(jnp.concatenate(split(rate * dt, 3), axis=0), tri_t[...])
    cs_t = sums[0:heads] + sums[heads : 2 * heads] + sums[2 * heads :]
    tail = jnp.exp(cs_t[:, span - 1 : span] - cs_t)
    rows_of = []
    for quantity in (dt, dt * tail, jnp.exp(cs_t)):
        rows_of += [term.astype(F32) for term in split(quantity, 2)]
    cs_wide = jnp.concatenate(rows_of + [cs_t, jnp.zeros_like(cs_t)], axis=0).T
    cs = cs_wide[:, 6 * heads : 7 * heads]
    wide_b = cs_wide.astype(BF16)
    for j in range(parts):
        ls = slice(j * LANES, (j + 1) * LANES)
        ecs[span - 8 : span, ls] = dot(wide_b[span - 16 : span], spread[j])[8:16, 2 * LANES :]

    theirs = cols(1 - odd, inner // 2)
    decay_swap = remote(
        ecs.at[span - 8 : span, theirs], pair_decay, d_sem.at[0], d_sem.at[1], pair, t
    )
    decay_swap.start()

    @pl.when(has_prev)
    def _():
        conv_recv.wait_recv()

    step_rows = 64
    for n in list(range(inner // LANES, wide // LANES)) + list(range(parts)):
        ns = slice(n * LANES, (n + 1) * LANES)
        if n < parts:
            scales = dot(wide_b, spread[n])
        for r in range(0, span, step_rows):
            rs = slice(r, r + step_rows)
            total = taps[0:1, ns] * ext[5 + r : 5 + r + step_rows, ns]
            for k in range(1, 4):
                total = total + taps[k : k + 1, ns] * ext[5 + k + r : 5 + k + r + step_rows, ns]
            x = total / (1.0 + jnp.exp(-total))
            xc[rs, ns] = x
            if n < parts:
                xdt[rs, ns] = (x * scales[rs, 0:LANES]).astype(BF16)
                xtail[rs, ns] = (x * scales[rs, LANES : 2 * LANES]).astype(BF16)
                if r + step_rows < span:
                    ecs[rs, ns] = scales[rs, 2 * LANES :]
                else:
                    ecs[r : span - 8, ns] = scales[r : span - 8, 2 * LANES :]

    b_t = xc[:, inner : inner + states].T.astype(BF16)
    c_b = xc[:, inner + states : wide].astype(BF16)

    def end_swap(i):
        return remote(x_out.at[i], x_in.at[i], x_send.at[i], x_recv.at[i], pair, t)

    def hand_down(i, cc):
        return remote(g_out.at[i], g_in.at[i], g_send.at[i], g_recv.at[i], cc, t)

    def share(i):
        j = odd * half + i
        return remote(p_out.at[i], st_in.at[j], p_send.at[i], p_recv.at[i], pair, t)

    def shared(i):
        j = (1 - odd) * half + i
        return remote(p_out.at[i], st_in.at[j], p_send.at[i], p_recv.at[i], pair, t)

    theirs_end = dot(b_t, xtail[:, theirs]).astype(BF16)
    for i in range(half):
        x_out[i] = theirs_end[:, i * LANES : (i + 1) * LANES]
        end_swap(i).start()
    mine_end = dot(b_t, xtail[:, cols(odd, inner // 2)])
    for i in range(half):
        end[i] = mine_end[:, i * LANES : (i + 1) * LANES]
    later = lax.broadcasted_iota(jnp.int32, (span, span), 0)
    earlier = lax.broadcasted_iota(jnp.int32, (span, span), 1)
    score[...] = jnp.where(later >= earlier, dot(c_b, b_t), 0.0)
    decay_swap.wait_recv()

    def relay():
        def part_of(i, _):
            ls = cols(i, LANES)
            mine = ecs[span - 8 : span, cols(odd * half + i, LANES)][7:8, :]
            other = pair_decay[:, ls][7:8, :]
            end_swap(i).wait_recv()
            end_mine = end[i]
            end_other = x_in[i].astype(F32)

            @pl.when(has_prev2)
            def _():
                hand_down(i, c - 2).wait_recv()

            even = odd == 0
            first = g_in[i].astype(F32)
            second = jnp.where(even, mine, other) * first + jnp.where(even, end_mine, end_other)

            @pl.when(has_next2)
            def _():
                after = jnp.where(even, other, mine) * second
                after = after + jnp.where(even, end_other, end_mine)
                g_out[i] = after.astype(BF16)
                hand_down(i, c + 2).start()

            p_out[i] = jnp.where(even, second, first).astype(BF16)
            share(i).start()
            st_in[odd * half + i] = jnp.where(even, first, second).astype(BF16)
            return 0

        lax.fori_loop(0, half, part_of, 0)

    @pl.when(c < 2)
    def _():
        relay()

    low_row = lax.broadcasted_iota(jnp.int32, (1, LANES), 1) < head_width
    low_head = lax.broadcasted_iota(jnp.int32, (LANES, LANES), 1) < head_width
    for j in range(parts):
        if j == parts // 2:

            @pl.when((c >= 2) & (c < 4))
            def _():
                relay()

        ls = slice(j * LANES, (j + 1) * LANES)
        for r in range(span // LANES):
            rs = slice(r * LANES, (r + 1) * LANES)
            upto = (r + 1) * LANES
            both = []
            for h in (2 * j, 2 * j + 1):
                diff = cs[rs, h : h + 1] - cs_t[h : h + 1, 0:upto]
                weights = score[rs, 0:upto] * jnp.exp(jnp.minimum(diff, 0.0))
                both.append(dot(weights.astype(BF16), xdt[0:upto, ls]))
            skip = jnp.where(low_row, skip_col[2 * j : 2 * j + 1], skip_col[2 * j + 1 : 2 * j + 2])
            yb[rs, ls] = jnp.where(low_head, both[0], both[1]) + skip * xc[rs, ls]

    @pl.when(c >= 4)
    def _():
        relay()

    same = (
        lax.broadcasted_iota(jnp.int32, (2 * LANES, LANES), 0) % LANES // head_width
        == lax.broadcasted_iota(jnp.int32, (2 * LANES, LANES), 1) // head_width
    )
    same = jnp.where(same, 1.0 / head_width, 0.0).astype(BF16)

    def finish_heads(j):
        ls = cols(j, LANES)
        y = yb[:, ls] + ecs[:, ls] * dot(c_b, st_in[j])
        mean_sq = dot(jnp.concatenate(split(y * y, 2), axis=1), same)
        normed[:, ls] = (y * lax.rsqrt(mean_sq + 1e-5) * gain[:, ls]).astype(BF16)

    for i in range(half):
        finish_heads(odd * half + i)
    for i in range(half):
        shared(i).wait_recv()
        finish_heads((1 - odd) * half + i)

    load_out.wait()

    def hop1(j):
        return remote(send1.at[j], recv1.at[j], r1_send.at[j], r1_recv.at[j], c, mate)

    def hop2(j):
        return remote(send2.at[j], recv2.at[j], r2_send.at[j], r2_recv.at[j], c, across)

    def multiply(j):
        prod = dot(normed[...], w_out[:, cols(j, oc)])
        part[...] = prod.reshape(4, rows, oc)
        send1[j, 0] = part[far].astype(BF16)
        send1[j, 1] = part[mate].astype(BF16)
        hop1(j).start()
        own[j, 0] = part[across]
        own[j, 1] = part[t]

    def pass_on(j):
        hop1(j).wait_recv()
        send2[j] = (own[j, 0] + recv1[j, 0].astype(F32)).astype(BF16)
        hop2(j).start()

    multiply(0)

    def step(j, _):
        multiply(j)
        pass_on(j - 1)
        return 0

    lax.fori_loop(1, OUT_PARTS, step, 0)
    pass_on(OUT_PARTS - 1)

    def finish(j, _):
        hop2(j).wait_recv()
        total = own[j, 1] + recv1[j, 1].astype(F32) + recv2[j].astype(F32)
        out[:, cols(j, oc)] = total.astype(BF16)
        return 0

    lax.fori_loop(0, OUT_PARTS, finish, 0)

    def drain_k(k, _):
        copy_a(k).wait_send()
        copy_b(k).wait_send()
        copy_f(k).wait_send()
        return 0

    lax.fori_loop(0, K_PARTS, drain_k, 0)

    def drain_o(j, _):
        hop1(j).wait_send()
        hop2(j).wait_send()
        return 0

    lax.fori_loop(0, OUT_PARTS, drain_o, 0)

    decay_swap.wait_send()

    def drain_s(i, _):
        end_swap(i).wait_send()
        share(i).wait_send()
        return 0

    lax.fori_loop(0, half, drain_s, 0)

    @pl.when(has_next)
    def _():
        conv_send.wait_send()

    @pl.when(has_next2)
    def _():
        def drain_g(i, _):
            hand_down(i, c + 2).wait_send()
            return 0

        lax.fori_loop(0, half, drain_g, 0)


def per_device(
    ctx_size, tokens, in_x, in_bc, in_dt, conv_x, conv_bc, dt_bias, a_log, skip_d, norm_gain, out_w
):
    rows, depth = tokens.shape
    span = 4 * rows
    inner = in_x.shape[1]
    wide = inner + in_bc.shape[1]
    states = in_bc.shape[1] // 2
    heads = a_log.shape[0]
    parts = inner // LANES
    half = parts // 2
    oc = depth // OUT_PARTS
    dma = pltpu.SemaphoreType.DMA
    anywhere = pl.BlockSpec(memory_space=pl.ANY)
    local = pl.BlockSpec(memory_space=pltpu.VMEM)
    return pl.pallas_call(
        functools.partial(layer_kernel, ctx_size),
        out_shape=jax.ShapeDtypeStruct((rows, depth), BF16),
        in_specs=[anywhere] * 5 + [local] * 6,
        out_specs=local,
        scratch_shapes=[
            pltpu.VMEM((4, rows, depth), BF16),
            pltpu.VMEM((depth, wide), BF16),
            pltpu.VMEM((heads, depth), BF16),
            pltpu.VMEM((inner, depth), BF16),
            pltpu.VMEM((span, wide), F32),
            pltpu.VMEM((heads, span), F32),
            pltpu.VMEM((span + 8, wide), F32),
            pltpu.VMEM((4, wide), F32),
            pltpu.VMEM((span, wide), F32),
            pltpu.VMEM((span, inner), BF16),
            pltpu.VMEM((span, inner), BF16),
            pltpu.VMEM((span, inner), F32),
            pltpu.VMEM((span, span), BF16),
            pltpu.VMEM((parts, 8 * heads, 3 * LANES), BF16),
            pltpu.VMEM((span, inner), F32),
            pltpu.VMEM((span, span), F32),
            pltpu.VMEM((half, states, LANES), F32),
            pltpu.VMEM((parts, states, LANES), BF16),
            pltpu.VMEM((half, states, LANES), BF16),
            pltpu.VMEM((half, states, LANES), BF16),
            pltpu.VMEM((half, states, LANES), BF16),
            pltpu.VMEM((half, states, LANES), BF16),
            pltpu.VMEM((half, states, LANES), BF16),
            pltpu.VMEM((8, inner // 2), F32),
            pltpu.VMEM((span, inner), BF16),
            pltpu.VMEM((4, rows, oc), F32),
            pltpu.VMEM((OUT_PARTS, 2, rows, oc), F32),
            pltpu.VMEM((OUT_PARTS, 2, rows, oc), BF16),
            pltpu.VMEM((OUT_PARTS, 2, rows, oc), BF16),
            pltpu.VMEM((OUT_PARTS, rows, oc), BF16),
            pltpu.VMEM((OUT_PARTS, rows, oc), BF16),
            dma((3, K_PARTS)),
            dma(()),
            dma((K_PARTS,)),
            dma((K_PARTS,)),
            dma((K_PARTS,)),
            dma((K_PARTS,)),
            dma((K_PARTS,)),
            dma((K_PARTS,)),
            dma((2,)),
            dma((2,)),
            dma((half,)),
            dma((half,)),
            dma((half,)),
            dma((half,)),
            dma((half,)),
            dma((half,)),
            dma((OUT_PARTS,)),
            dma((OUT_PARTS,)),
            dma((OUT_PARTS,)),
            dma((OUT_PARTS,)),
        ],
        compiler_params=pltpu.CompilerParams(
            collective_id=0, has_side_effects=True, vmem_limit_bytes=56 * 2**20
        ),
    )(
        tokens,
        in_x,
        in_bc,
        in_dt.T,
        out_w,
        conv_x,
        conv_bc,
        dt_bias.reshape(1, heads),
        a_log.reshape(1, heads),
        skip_d.reshape(1, heads),
        norm_gain.reshape(1, inner),
    )


def solution(mesh):
    return jax.shard_map(
        functools.partial(per_device, mesh.shape["ctx"]),
        mesh=mesh,
        in_specs=(
            P(("ctx", "tp"), None),
            P(None, "tp"),
            P(),
            P(None, "tp"),
            P(None, "tp"),
            P(),
            P("tp"),
            P("tp"),
            P("tp"),
            P("tp"),
            P("tp", None),
        ),
        out_specs=P(("ctx", "tp"), None),
        check_vma=False,
    )
```

```python
import functools

import jax
import jax.numpy as jnp
from jax import lax
from jax.experimental import pallas as pl
from jax.experimental.pallas import tpu as pltpu
from jax.sharding import PartitionSpec as P

MESH = pl.DeviceIdType.MESH
F32 = jnp.float32
BF16 = jnp.bfloat16
K_PARTS = 8
OUT_PARTS = 16
TILE = 256
LANES = 128


def dot(a, b):
    return jnp.dot(a, b, preferred_element_type=F32)


def split(v, parts):
    terms = []
    for _ in range(parts):
        term = v.astype(BF16)
        terms.append(term)
        v = v - term.astype(F32)
    return terms


def layer_kernel(
    ctx_size,
    tokens,
    in_x,
    in_bc,
    in_dt,
    out_w,
    conv_x,
    conv_bc,
    dt_bias,
    a_log,
    skip_d,
    gain,
    out,
    gath,
    w_in,
    w_dt,
    w_out,
    acc,
    acc_dt,
    ext,
    taps,
    xc,
    xdt,
    xtail,
    ecs,
    tri_t,
    spread,
    yb,
    score,
    end,
    st_in,
    x_out,
    x_in,
    g_out,
    g_in,
    p_out,
    pair_decay,
    normed,
    part,
    own,
    send1,
    recv1,
    send2,
    recv2,
    load_sem,
    tok_sem,
    a_send,
    a_recv,
    b_send,
    b_recv,
    f_send,
    f_recv,
    conv_sem,
    d_sem,
    x_send,
    x_recv,
    g_send,
    g_recv,
    p_send,
    p_recv,
    r1_send,
    r1_recv,
    r2_send,
    r2_recv,
):
    c = lax.axis_index("ctx")
    t = lax.axis_index("tp")
    mate = t + 1 - 2 * (t % 2)
    across = (t + 2) % 4
    far = (mate + 2) % 4
    rows, depth = tokens.shape
    span = 4 * rows
    inner = in_x.shape[1]
    bc = in_bc.shape[1]
    wide = inner + bc
    states = bc // 2
    heads = dt_bias.shape[1]
    kc = depth // K_PARTS
    oc = depth // OUT_PARTS
    has_prev = c > 0
    has_next = c < ctx_size - 1
    has_prev2 = c > 1
    has_next2 = c < ctx_size - 2
    odd = c % 2
    pair = c + 1 - 2 * odd
    parts = inner // LANES
    half = parts // 2

    def cols(i, size):
        return pl.ds(pl.multiple_of(i * size, size), size)

    def load(k):
        ks = cols(k, kc)
        return (
            pltpu.make_async_copy(in_x.at[ks, :], w_in.at[ks, 0:inner], load_sem.at[0, k]),
            pltpu.make_async_copy(in_bc.at[ks, :], w_in.at[ks, inner:wide], load_sem.at[1, k]),
        )

    load_dt = pltpu.make_async_copy(in_dt, w_dt, load_sem.at[2, 0])
    load_out = pltpu.make_async_copy(out_w, w_out, load_sem.at[2, 1])
    load_tok = pltpu.make_async_copy(tokens, gath.at[t], tok_sem)

    def remote(src, dst, send, recv, cc, tt):
        return pltpu.make_async_remote_copy(
            src_ref=src,
            dst_ref=dst,
            send_sem=send,
            recv_sem=recv,
            device_id=(cc, tt),
            device_id_type=MESH,
        )

    def copy_a(k):
        ks = cols(k, kc)
        return remote(
            tokens.at[:, ks], gath.at[t, :, ks], a_send.at[k], a_recv.at[k], c, across
        )

    def copy_b(k):
        ks = cols(k, kc)
        return remote(tokens.at[:, ks], gath.at[t, :, ks], b_send.at[k], b_recv.at[k], c, mate)

    def copy_f(k):
        ks = cols(k, kc)
        return remote(
            gath.at[across, :, ks], gath.at[across, :, ks], f_send.at[k], f_recv.at[k], c, mate
        )

    def got(block, k, send, recv):
        ks = cols(k, kc)
        return remote(
            gath.at[block, :, ks], gath.at[block, :, ks], send.at[k], recv.at[k], c, mate
        )

    barrier = pltpu.get_barrier_semaphore()
    for tt in (mate, across):
        pl.semaphore_signal(barrier, inc=1, device_id=(c, tt), device_id_type=MESH)

    @pl.when(has_prev)
    def _():
        pl.semaphore_signal(barrier, inc=1, device_id=(c - 1, t), device_id_type=MESH)

    @pl.when(has_next)
    def _():
        pl.semaphore_signal(barrier, inc=1, device_id=(c + 1, t), device_id_type=MESH)

    @pl.when(has_prev2)
    def _():
        pl.semaphore_signal(barrier, inc=1, device_id=(c - 2, t), device_id_type=MESH)

    @pl.when(has_next2)
    def _():
        pl.semaphore_signal(barrier, inc=1, device_id=(c + 2, t), device_id_type=MESH)

    load_tok.start()
    load_dt.start()
    for k in range(K_PARTS):
        for copy in load(k):
            copy.start()

    peers = 2
    for flag in (has_prev, has_next, has_prev2, has_next2):
        peers = peers + jnp.where(flag, 1, 0)
    pl.semaphore_wait(barrier, peers)

    for k in range(K_PARTS):
        copy_a(k).start()
    for k in range(K_PARTS):
        copy_b(k).start()

    taps[:, 0:inner] = conv_x[...]
    taps[:, inner:wide] = conv_bc[...]
    acc[...] = jnp.zeros_like(acc)
    acc_dt[...] = jnp.zeros_like(acc_dt)

    @pl.when(c == 0)
    def _():
        ext[0:8, :] = jnp.zeros((8, wide), F32)

    @pl.when(c < 2)
    def _():
        g_in[...] = jnp.zeros_like(g_in)

    head_width = inner // heads
    fields = 8 * heads
    earlier = lax.broadcasted_iota(jnp.int32, (span, span), 0)
    later = lax.broadcasted_iota(jnp.int32, (span, span), 1)
    tri_t[...] = jnp.where(later >= earlier, 1.0, 0.0).astype(BF16)
    field = lax.broadcasted_iota(jnp.int32, (fields, 3 * LANES), 0)
    lane = lax.broadcasted_iota(jnp.int32, (fields, 3 * LANES), 1)
    for j in range(parts):
        head = (lane % LANES + j * LANES) // head_width
        hit = (field % heads == head) & (field // (2 * heads) == lane // LANES)
        spread[j] = jnp.where(hit, 1.0, 0.0).astype(BF16)
    eye = lax.broadcasted_iota(jnp.int32, (heads, heads), 0) == lax.broadcasted_iota(
        jnp.int32, (heads, heads), 1
    )

    def upright(row):
        return jnp.sum(jnp.where(eye, row, 0.0), axis=1, keepdims=True)

    bias = upright(dt_bias[...])
    rate = -jnp.exp(upright(a_log[...]))
    skip_col = jnp.broadcast_to(upright(skip_d[...]), (heads, LANES))

    load_tok.wait()
    load_dt.wait()

    def project(k, _):
        ks = cols(k, kc)
        got(across, k, a_send, a_recv).wait_recv()
        copy_f(k).start()
        got(mate, k, b_send, b_recv).wait_recv()
        for copy in load(k):
            copy.wait()
        got(far, k, f_send, f_recv).wait_recv()
        lhs = gath[:, :, ks].reshape(span, kc)
        acc_dt[...] += lax.dot_general(
            w_dt[:, ks], lhs, (((1,), (1,)), ((), ())), preferred_element_type=F32
        )

        for n in range(wide // TILE):
            ns = slice(n * TILE, (n + 1) * TILE)
            acc[:, ns] += dot(lhs, w_in[ks, ns])
        return 0

    lax.fori_loop(0, K_PARTS, project, 0)
    load_out.start()

    ext[span : span + 8, :] = acc[span - 8 : span, :].astype(BF16).astype(F32)
    conv_send = remote(
        ext.at[span : span + 8, :], ext.at[0:8, :], conv_sem.at[0], conv_sem.at[1], c + 1, t
    )
    conv_recv = remote(
        ext.at[span : span + 8, :], ext.at[0:8, :], conv_sem.at[0], conv_sem.at[1], c - 1, t
    )

    @pl.when(has_next)
    def _():
        conv_send.start()

    for n in range(wide // TILE):
        ns = slice(n * TILE, (n + 1) * TILE)
        ext[8:span, ns] = acc[0 : span - 8, ns].astype(BF16).astype(F32)

    v = acc_dt[...] + bias
    dt = jnp.maximum(v, 0.0) + jnp.log1p(jnp.exp(-jnp.abs(v)))
    sums = dot(jnp.concatenate(split(rate * dt, 3), axis=0), tri_t[...])
    cs_t = sums[0:heads] + sums[heads : 2 * heads] + sums[2 * heads :]
    tail = jnp.exp(cs_t[:, span - 1 : span] - cs_t)
    rows_of = []
    for quantity in (dt, dt * tail, jnp.exp(cs_t)):
        rows_of += [term.astype(F32) for term in split(quantity, 2)]
    cs_wide = jnp.concatenate(rows_of + [cs_t, jnp.zeros_like(cs_t)], axis=0).T
    cs = cs_wide[:, 6 * heads : 7 * heads]
    wide_b = cs_wide.astype(BF16)
    for j in range(parts):
        ls = slice(j * LANES, (j + 1) * LANES)
        ecs[span - 8 : span, ls] = dot(wide_b[span - 16 : span], spread[j])[8:16, 2 * LANES :]

    theirs = cols(1 - odd, inner // 2)
    decay_swap = remote(
        ecs.at[span - 8 : span, theirs], pair_decay, d_sem.at[0], d_sem.at[1], pair, t
    )
    decay_swap.start()

    step_rows = 64

    def conv(ns, r, scales):
        rs = slice(r, r + step_rows)
        total = taps[0:1, ns] * ext[5 + r : 5 + r + step_rows, ns]
        for k in range(1, 4):
            total = total + taps[k : k + 1, ns] * ext[5 + k + r : 5 + k + r + step_rows, ns]
        x = total / (1.0 + jnp.exp(-total))
        xc[rs, ns] = x
        if scales is not None:
            xdt[rs, ns] = (x * scales[rs, 0:LANES]).astype(BF16)
            xtail[rs, ns] = (x * scales[rs, LANES : 2 * LANES]).astype(BF16)
            upto = min(r + step_rows, span - 8)
            ecs[r:upto, ns] = scales[r:upto, 2 * LANES :]

    bc_tiles = [slice(n, n + LANES) for n in range(inner, wide, LANES)]
    for ns in bc_tiles:
        for r in range(step_rows, span, step_rows):
            conv(ns, r, None)
    tiles = []
    for i in range(half):
        n = (1 - odd) * half + i
        scales = dot(wide_b, spread[n])
        tiles.append((cols(n, LANES), scales))
        for r in range(step_rows, span, step_rows):
            conv(cols(n, LANES), r, scales)

    @pl.when(has_prev)
    def _():
        conv_recv.wait_recv()

    for ns in bc_tiles:
        conv(ns, 0, None)
    for ns, scales in tiles:
        conv(ns, 0, scales)

    b_t = xc[:, inner : inner + states].T.astype(BF16)
    c_b = xc[:, inner + states : wide].astype(BF16)

    def end_swap(i):
        return remote(x_out.at[i], x_in.at[i], x_send.at[i], x_recv.at[i], pair, t)

    def hand_down(i, cc):
        return remote(g_out.at[i], g_in.at[i], g_send.at[i], g_recv.at[i], cc, t)

    def share(i):
        j = odd * 2 * half + i
        return remote(p_out.at[i], st_in.at[j], p_send.at[i], p_recv.at[i], pair, t)

    def shared(i):
        j = (1 - odd) * 2 * half + i
        return remote(p_out.at[i], st_in.at[j], p_send.at[i], p_recv.at[i], pair, t)

    theirs_end = dot(b_t, xtail[:, theirs]).astype(BF16)
    low = states // 2
    pieces = 2 * half

    def cut_up(whole):
        for i in range(pieces):
            yield whole[(i % 2) * low : (i % 2 + 1) * low, i // 2 * LANES : (i // 2 + 1) * LANES]

    for i, piece in enumerate(cut_up(theirs_end)):
        x_out[i] = piece
        end_swap(i).start()
    for i in range(half):
        n = odd * half + i
        scales = dot(wide_b, spread[n])
        for r in range(0, span, step_rows):
            conv(cols(n, LANES), r, scales)
    mine_end = dot(b_t, xtail[:, cols(odd, inner // 2)])
    for i, piece in enumerate(cut_up(mine_end)):
        end[i] = piece
    later = lax.broadcasted_iota(jnp.int32, (span, span), 0)
    earlier = lax.broadcasted_iota(jnp.int32, (span, span), 1)
    score[...] = jnp.where(later >= earlier, dot(c_b, b_t), 0.0)
    decay_swap.wait_recv()

    def relay():
        def part_of(i, _):
            ls = cols(i // 2, LANES)
            mine = ecs[span - 8 : span, cols(odd * half + i // 2, LANES)][7:8, :]
            other = pair_decay[:, ls][7:8, :]
            end_swap(i).wait_recv()
            end_mine = end[i]
            end_other = x_in[i].astype(F32)

            @pl.when(has_prev2)
            def _():
                hand_down(i, c - 2).wait_recv()

            even = odd == 0
            first = g_in[i].astype(F32)
            second = jnp.where(even, mine, other) * first + jnp.where(even, end_mine, end_other)

            @pl.when(has_next2)
            def _():
                after = jnp.where(even, other, mine) * second
                after = after + jnp.where(even, end_other, end_mine)
                g_out[i] = after.astype(BF16)
                hand_down(i, c + 2).start()

            p_out[i] = jnp.where(even, second, first).astype(BF16)
            share(i).start()
            st_in[odd * pieces + i] = jnp.where(even, first, second).astype(BF16)
            return 0

        lax.fori_loop(0, pieces, part_of, 0)

    @pl.when(c < 2)
    def _():
        relay()

    low_row = lax.broadcasted_iota(jnp.int32, (1, LANES), 1) < head_width
    low_head = lax.broadcasted_iota(jnp.int32, (LANES, LANES), 1) < head_width
    for j in range(parts):
        if j == parts // 2:

            @pl.when((c >= 2) & (c < 4))
            def _():
                relay()

        ls = slice(j * LANES, (j + 1) * LANES)
        for r in range(span // LANES):
            rs = slice(r * LANES, (r + 1) * LANES)
            upto = (r + 1) * LANES
            both = []
            for h in (2 * j, 2 * j + 1):
                diff = cs[rs, h : h + 1] - cs_t[h : h + 1, 0:upto]
                weights = score[rs, 0:upto] * jnp.exp(jnp.minimum(diff, 0.0))
                both.append(dot(weights.astype(BF16), xdt[0:upto, ls]))
            skip = jnp.where(low_row, skip_col[2 * j : 2 * j + 1], skip_col[2 * j + 1 : 2 * j + 2])
            yb[rs, ls] = jnp.where(low_head, both[0], both[1]) + skip * xc[rs, ls]

    @pl.when(c >= 4)
    def _():
        relay()

    same = (
        lax.broadcasted_iota(jnp.int32, (2 * LANES, LANES), 0) % LANES // head_width
        == lax.broadcasted_iota(jnp.int32, (2 * LANES, LANES), 1) // head_width
    )
    same = jnp.where(same, 1.0 / head_width, 0.0).astype(BF16)

    def finish_heads(j):
        ls = cols(j, LANES)
        state = st_in[pl.ds(2 * j, 2)].reshape(states, LANES)
        y = yb[:, ls] + ecs[:, ls] * dot(c_b, state)
        mean_sq = dot(jnp.concatenate(split(y * y, 2), axis=1), same)
        normed[:, ls] = (y * lax.rsqrt(mean_sq + 1e-5) * gain[:, ls]).astype(BF16)

    for i in range(half):
        finish_heads(odd * half + i)
    for i in range(half):
        shared(2 * i).wait_recv()
        shared(2 * i + 1).wait_recv()
        finish_heads((1 - odd) * half + i)

    load_out.wait()

    def hop1(j):
        return remote(send1.at[j], recv1.at[j], r1_send.at[j], r1_recv.at[j], c, mate)

    def hop2(j):
        return remote(send2.at[j], recv2.at[j], r2_send.at[j], r2_recv.at[j], c, across)

    def multiply(j):
        prod = dot(normed[...], w_out[:, cols(j, oc)])
        part[...] = prod.reshape(4, rows, oc)
        send1[j, 0] = part[far].astype(BF16)
        send1[j, 1] = part[mate].astype(BF16)
        hop1(j).start()
        own[j, 0] = part[across]
        own[j, 1] = part[t]

    def pass_on(j):
        hop1(j).wait_recv()
        send2[j] = (own[j, 0] + recv1[j, 0].astype(F32)).astype(BF16)
        hop2(j).start()

    multiply(0)

    def step(j, _):
        multiply(j)
        pass_on(j - 1)
        return 0

    lax.fori_loop(1, OUT_PARTS, step, 0)
    pass_on(OUT_PARTS - 1)

    def finish(j, _):
        hop2(j).wait_recv()
        total = own[j, 1] + recv1[j, 1].astype(F32) + recv2[j].astype(F32)
        out[:, cols(j, oc)] = total.astype(BF16)
        return 0

    lax.fori_loop(0, OUT_PARTS, finish, 0)

    def drain_k(k, _):
        copy_a(k).wait_send()
        copy_b(k).wait_send()
        copy_f(k).wait_send()
        return 0

    lax.fori_loop(0, K_PARTS, drain_k, 0)

    def drain_o(j, _):
        hop1(j).wait_send()
        hop2(j).wait_send()
        return 0

    lax.fori_loop(0, OUT_PARTS, drain_o, 0)

    decay_swap.wait_send()

    def drain_s(i, _):
        end_swap(i).wait_send()
        share(i).wait_send()
        return 0

    lax.fori_loop(0, pieces, drain_s, 0)

    @pl.when(has_next)
    def _():
        conv_send.wait_send()

    @pl.when(has_next2)
    def _():
        def drain_g(i, _):
            hand_down(i, c + 2).wait_send()
            return 0

        lax.fori_loop(0, pieces, drain_g, 0)


def per_device(
    ctx_size, tokens, in_x, in_bc, in_dt, conv_x, conv_bc, dt_bias, a_log, skip_d, norm_gain, out_w
):
    rows, depth = tokens.shape
    span = 4 * rows
    inner = in_x.shape[1]
    wide = inner + in_bc.shape[1]
    states = in_bc.shape[1] // 2
    heads = a_log.shape[0]
    parts = inner // LANES
    half = parts // 2
    oc = depth // OUT_PARTS
    dma = pltpu.SemaphoreType.DMA
    anywhere = pl.BlockSpec(memory_space=pl.ANY)
    local = pl.BlockSpec(memory_space=pltpu.VMEM)
    return pl.pallas_call(
        functools.partial(layer_kernel, ctx_size),
        out_shape=jax.ShapeDtypeStruct((rows, depth), BF16),
        in_specs=[anywhere] * 5 + [local] * 6,
        out_specs=local,
        scratch_shapes=[
            pltpu.VMEM((4, rows, depth), BF16),
            pltpu.VMEM((depth, wide), BF16),
            pltpu.VMEM((heads, depth), BF16),
            pltpu.VMEM((inner, depth), BF16),
            pltpu.VMEM((span, wide), F32),
            pltpu.VMEM((heads, span), F32),
            pltpu.VMEM((span + 8, wide), F32),
            pltpu.VMEM((4, wide), F32),
            pltpu.VMEM((span, wide), F32),
            pltpu.VMEM((span, inner), BF16),
            pltpu.VMEM((span, inner), BF16),
            pltpu.VMEM((span, inner), F32),
            pltpu.VMEM((span, span), BF16),
            pltpu.VMEM((parts, 8 * heads, 3 * LANES), BF16),
            pltpu.VMEM((span, inner), F32),
            pltpu.VMEM((span, span), F32),
            pltpu.VMEM((2 * half, states // 2, LANES), F32),
            pltpu.VMEM((2 * parts, states // 2, LANES), BF16),
            pltpu.VMEM((2 * half, states // 2, LANES), BF16),
            pltpu.VMEM((2 * half, states // 2, LANES), BF16),
            pltpu.VMEM((2 * half, states // 2, LANES), BF16),
            pltpu.VMEM((2 * half, states // 2, LANES), BF16),
            pltpu.VMEM((2 * half, states // 2, LANES), BF16),
            pltpu.VMEM((8, inner // 2), F32),
            pltpu.VMEM((span, inner), BF16),
            pltpu.VMEM((4, rows, oc), F32),
            pltpu.VMEM((OUT_PARTS, 2, rows, oc), F32),
            pltpu.VMEM((OUT_PARTS, 2, rows, oc), BF16),
            pltpu.VMEM((OUT_PARTS, 2, rows, oc), BF16),
            pltpu.VMEM((OUT_PARTS, rows, oc), BF16),
            pltpu.VMEM((OUT_PARTS, rows, oc), BF16),
            dma((3, K_PARTS)),
            dma(()),
            dma((K_PARTS,)),
            dma((K_PARTS,)),
            dma((K_PARTS,)),
            dma((K_PARTS,)),
            dma((K_PARTS,)),
            dma((K_PARTS,)),
            dma((2,)),
            dma((2,)),
            dma((2 * half,)),
            dma((2 * half,)),
            dma((2 * half,)),
            dma((2 * half,)),
            dma((2 * half,)),
            dma((2 * half,)),
            dma((OUT_PARTS,)),
            dma((OUT_PARTS,)),
            dma((OUT_PARTS,)),
            dma((OUT_PARTS,)),
        ],
        compiler_params=pltpu.CompilerParams(
            collective_id=0, has_side_effects=True, vmem_limit_bytes=56 * 2**20
        ),
    )(
        tokens,
        in_x,
        in_bc,
        in_dt.T,
        out_w,
        conv_x,
        conv_bc,
        dt_bias.reshape(1, heads),
        a_log.reshape(1, heads),
        skip_d.reshape(1, heads),
        norm_gain.reshape(1, inner),
    )


def solution(mesh):
    return jax.shard_map(
        functools.partial(per_device, mesh.shape["ctx"]),
        mesh=mesh,
        in_specs=(
            P(("ctx", "tp"), None),
            P(None, "tp"),
            P(),
            P(None, "tp"),
            P(None, "tp"),
            P(),
            P("tp"),
            P("tp"),
            P("tp"),
            P("tp"),
            P("tp", None),
        ),
        out_specs=P(("ctx", "tp"), None),
        check_vma=False,
    )
```

```python
import functools

import jax
import jax.numpy as jnp
from jax import lax
from jax.experimental import pallas as pl
from jax.experimental.pallas import tpu as pltpu
from jax.sharding import PartitionSpec as P

MESH = pl.DeviceIdType.MESH
F32 = jnp.float32
BF16 = jnp.bfloat16
K_PARTS = 8
OUT_PARTS = 16
TILE = 256
LANES = 128
LAG = 2


def dot(a, b):
    return jnp.dot(a, b, preferred_element_type=F32)


def split(v, parts):
    terms = []
    for _ in range(parts):
        term = v.astype(BF16)
        terms.append(term)
        v = v - term.astype(F32)
    return terms


def layer_kernel(
    ctx_size,
    tokens,
    in_x,
    in_bc,
    in_dt,
    out_w,
    conv_x,
    conv_bc,
    dt_bias_in,
    a_log_in,
    skip_d_in,
    gain_in,
    out,
    dt_bias,
    a_log,
    skip_d,
    gain,
    staged,
    gath,
    w_in,
    w_dt,
    w_out,
    acc,
    acc_dt,
    ext,
    taps,
    xc,
    xdt,
    xtail,
    ecs,
    tri_t,
    spread,
    yb,
    score,
    end,
    st_in,
    x_out,
    x_in,
    g_out,
    g_in,
    p_out,
    pair_decay,
    normed,
    part,
    own,
    send1,
    recv1,
    send2,
    recv2,
    small_sem,
    out_sem,
    load_sem,
    tok_sem,
    a_send,
    a_recv,
    b_send,
    b_recv,
    f_send,
    f_recv,
    conv_sem,
    d_sem,
    x_send,
    x_recv,
    g_send,
    g_recv,
    p_send,
    p_recv,
    r1_send,
    r1_recv,
    r2_send,
    r2_recv,
):
    c = lax.axis_index("ctx")
    t = lax.axis_index("tp")
    mate = t + 1 - 2 * (t % 2)
    across = (t + 2) % 4
    far = (mate + 2) % 4
    rows, depth = tokens.shape
    span = 4 * rows
    inner = in_x.shape[1]
    bc = in_bc.shape[1]
    wide = inner + bc
    states = bc // 2
    heads = dt_bias_in.shape[1]
    kc = depth // K_PARTS
    oc = depth // OUT_PARTS
    has_prev = c > 0
    has_next = c < ctx_size - 1
    has_prev2 = c > 1
    has_next2 = c < ctx_size - 2
    odd = c % 2
    pair = c + 1 - 2 * odd
    parts = inner // LANES
    half = parts // 2

    def cols(i, size):
        return pl.ds(pl.multiple_of(i * size, size), size)

    def load(k):
        ks = cols(k, kc)
        return (
            pltpu.make_async_copy(in_x.at[ks, :], w_in.at[ks, 0:inner], load_sem.at[0, k]),
            pltpu.make_async_copy(in_bc.at[ks, :], w_in.at[ks, inner:wide], load_sem.at[1, k]),
        )

    load_dt = pltpu.make_async_copy(in_dt, w_dt, load_sem.at[2, 0])
    load_out = pltpu.make_async_copy(out_w, w_out, load_sem.at[2, 1])
    load_tok = pltpu.make_async_copy(tokens, gath.at[t], tok_sem)

    def remote(src, dst, send, recv, cc, tt):
        return pltpu.make_async_remote_copy(
            src_ref=src,
            dst_ref=dst,
            send_sem=send,
            recv_sem=recv,
            device_id=(cc, tt),
            device_id_type=MESH,
        )

    def copy_a(k):
        ks = cols(k, kc)
        return remote(
            tokens.at[:, ks], gath.at[t, :, ks], a_send.at[k], a_recv.at[k], c, across
        )

    def copy_b(k):
        ks = cols(k, kc)
        return remote(tokens.at[:, ks], gath.at[t, :, ks], b_send.at[k], b_recv.at[k], c, mate)

    def copy_f(k):
        ks = cols(k, kc)
        return remote(
            gath.at[across, :, ks], gath.at[across, :, ks], f_send.at[k], f_recv.at[k], c, mate
        )

    def got(block, k, send, recv):
        ks = cols(k, kc)
        return remote(
            gath.at[block, :, ks], gath.at[block, :, ks], send.at[k], recv.at[k], c, mate
        )

    barrier = pltpu.get_barrier_semaphore()
    for tt in (mate, across):
        pl.semaphore_signal(barrier, inc=1, device_id=(c, tt), device_id_type=MESH)

    @pl.when(has_prev)
    def _():
        pl.semaphore_signal(barrier, inc=1, device_id=(c - 1, t), device_id_type=MESH)

    @pl.when(has_next)
    def _():
        pl.semaphore_signal(barrier, inc=1, device_id=(c + 1, t), device_id_type=MESH)

    @pl.when(has_prev2)
    def _():
        pl.semaphore_signal(barrier, inc=1, device_id=(c - 2, t), device_id_type=MESH)

    @pl.when(has_next2)
    def _():
        pl.semaphore_signal(barrier, inc=1, device_id=(c + 2, t), device_id_type=MESH)

    load_tok.start()
    load_dt.start()
    small = [
        pltpu.make_async_copy(src, dst, small_sem.at[i])
        for i, (src, dst) in enumerate(
            (
                (conv_x, taps.at[:, 0:inner]),
                (conv_bc, taps.at[:, inner:wide]),
                (dt_bias_in, dt_bias),
                (a_log_in, a_log),
                (skip_d_in, skip_d),
                (gain_in, gain),
            )
        )
    ]
    for copy in small:
        copy.start()
    for k in range(K_PARTS):
        for copy in load(k):
            copy.start()

    peers = 2
    for flag in (has_prev, has_next, has_prev2, has_next2):
        peers = peers + jnp.where(flag, 1, 0)
    pl.semaphore_wait(barrier, peers)

    for k in range(K_PARTS):
        copy_a(k).start()
    for k in range(K_PARTS):
        copy_b(k).start()

    acc[...] = jnp.zeros_like(acc)
    acc_dt[...] = jnp.zeros_like(acc_dt)

    @pl.when(c == 0)
    def _():
        ext[0:8, :] = jnp.zeros((8, wide), F32)

    @pl.when(c < 2)
    def _():
        g_in[...] = jnp.zeros_like(g_in)

    head_width = inner // heads
    fields = 8 * heads
    earlier = lax.broadcasted_iota(jnp.int32, (span, span), 0)
    later = lax.broadcasted_iota(jnp.int32, (span, span), 1)
    tri_t[...] = jnp.where(later >= earlier, 1.0, 0.0).astype(BF16)
    field = lax.broadcasted_iota(jnp.int32, (fields, 3 * LANES), 0)
    lane = lax.broadcasted_iota(jnp.int32, (fields, 3 * LANES), 1)
    for j in range(parts):
        head = (lane % LANES + j * LANES) // head_width
        hit = (field % heads == head) & (field // (2 * heads) == lane // LANES)
        spread[j] = jnp.where(hit, 1.0, 0.0).astype(BF16)
    eye = lax.broadcasted_iota(jnp.int32, (heads, heads), 0) == lax.broadcasted_iota(
        jnp.int32, (heads, heads), 1
    )

    def upright(row):
        return jnp.sum(jnp.where(eye, row, 0.0), axis=1, keepdims=True)

    for copy in small:
        copy.wait()
    bias = upright(dt_bias[...])
    rate = -jnp.exp(upright(a_log[...]))
    skip_col = jnp.broadcast_to(upright(skip_d[...]), (heads, LANES))

    load_tok.wait()
    load_dt.wait()

    def forward(k):
        got(across, k, a_send, a_recv).wait_recv()
        copy_f(k).start()

    def project(k):
        ks = cols(k, kc)
        got(mate, k, b_send, b_recv).wait_recv()
        for copy in load(k):
            copy.wait()
        got(far, k, f_send, f_recv).wait_recv()
        lhs = gath[:, :, ks].reshape(span, kc)
        acc_dt[...] += lax.dot_general(
            w_dt[:, ks], lhs, (((1,), (1,)), ((), ())), preferred_element_type=F32
        )

        for n in range(wide // TILE):
            ns = slice(n * TILE, (n + 1) * TILE)
            acc[:, ns] += dot(lhs, w_in[ks, ns])

    def gather_step(k, _):
        forward(k)
        project(k - 1)
        return 0

    forward(0)
    lax.fori_loop(1, K_PARTS, gather_step, 0)
    project(K_PARTS - 1)
    load_out.start()

    ext[span : span + 8, :] = acc[span - 8 : span, :].astype(BF16).astype(F32)
    conv_send = remote(
        ext.at[span : span + 8, :], ext.at[0:8, :], conv_sem.at[0], conv_sem.at[1], c + 1, t
    )
    conv_recv = remote(
        ext.at[span : span + 8, :], ext.at[0:8, :], conv_sem.at[0], conv_sem.at[1], c - 1, t
    )

    @pl.when(has_next)
    def _():
        conv_send.start()

    for n in range(wide // TILE):
        ns = slice(n * TILE, (n + 1) * TILE)
        ext[8:span, ns] = acc[0 : span - 8, ns].astype(BF16).astype(F32)

    v = acc_dt[...] + bias
    dt = jnp.maximum(v, 0.0) + jnp.log1p(jnp.exp(-jnp.abs(v)))
    sums = dot(jnp.concatenate(split(rate * dt, 3), axis=0), tri_t[...])
    cs_t = sums[0:heads] + sums[heads : 2 * heads] + sums[2 * heads :]
    tail = jnp.exp(cs_t[:, span - 1 : span] - cs_t)
    rows_of = []
    for quantity in (dt, dt * tail, jnp.exp(cs_t)):
        rows_of += [term.astype(F32) for term in split(quantity, 2)]
    cs_wide = jnp.concatenate(rows_of + [cs_t, jnp.zeros_like(cs_t)], axis=0).T
    cs = cs_wide[:, 6 * heads : 7 * heads]
    wide_b = cs_wide.astype(BF16)
    for j in range(parts):
        ls = slice(j * LANES, (j + 1) * LANES)
        ecs[span - 8 : span, ls] = dot(wide_b[span - 16 : span], spread[j])[8:16, 2 * LANES :]

    theirs = cols(1 - odd, inner // 2)
    decay_swap = remote(
        ecs.at[span - 8 : span, theirs], pair_decay, d_sem.at[0], d_sem.at[1], pair, t
    )
    decay_swap.start()

    step_rows = 64

    def conv(ns, r, scales):
        rs = slice(r, r + step_rows)
        total = taps[0:1, ns] * ext[5 + r : 5 + r + step_rows, ns]
        for k in range(1, 4):
            total = total + taps[k : k + 1, ns] * ext[5 + k + r : 5 + k + r + step_rows, ns]
        x = 0.5 * total
        x = x * jnp.tanh(x) + x
        xc[rs, ns] = x
        if scales is not None:
            xdt[rs, ns] = (x * scales[rs, 0:LANES]).astype(BF16)
            xtail[rs, ns] = (x * scales[rs, LANES : 2 * LANES]).astype(BF16)
            upto = min(r + step_rows, span - 8)
            ecs[r:upto, ns] = scales[r:upto, 2 * LANES :]

    bc_tiles = [slice(n, n + LANES) for n in range(inner, wide, LANES)]
    for ns in bc_tiles:
        for r in range(step_rows, span, step_rows):
            conv(ns, r, None)
    tiles = []
    for i in range(half):
        n = (1 - odd) * half + i
        scales = dot(wide_b, spread[n])
        tiles.append((cols(n, LANES), scales))
        for r in range(step_rows, span, step_rows):
            conv(cols(n, LANES), r, scales)

    @pl.when(has_prev)
    def _():
        conv_recv.wait_recv()

    for ns in bc_tiles:
        conv(ns, 0, None)
    for ns, scales in tiles:
        conv(ns, 0, scales)

    b_t = xc[:, inner : inner + states].T.astype(BF16)
    c_b = xc[:, inner + states : wide].astype(BF16)

    def end_swap(i):
        return remote(x_out.at[i], x_in.at[i], x_send.at[i], x_recv.at[i], pair, t)

    def hand_down(i, cc):
        return remote(g_out.at[i], g_in.at[i], g_send.at[i], g_recv.at[i], cc, t)

    def share(i):
        j = odd * 2 * half + i
        return remote(p_out.at[i], st_in.at[j], p_send.at[i], p_recv.at[i], pair, t)

    def shared(i):
        j = (1 - odd) * 2 * half + i
        return remote(p_out.at[i], st_in.at[j], p_send.at[i], p_recv.at[i], pair, t)

    theirs_end = dot(b_t, xtail[:, theirs]).astype(BF16)
    low = states // 2
    pieces = 2 * half

    def cut_up(whole):
        for i in range(pieces):
            yield whole[(i % 2) * low : (i % 2 + 1) * low, i // 2 * LANES : (i // 2 + 1) * LANES]

    for i, piece in enumerate(cut_up(theirs_end)):
        x_out[i] = piece
        end_swap(i).start()
    for i in range(half):
        n = odd * half + i
        scales = dot(wide_b, spread[n])
        for r in range(0, span, step_rows):
            conv(cols(n, LANES), r, scales)
    mine_end = dot(b_t, xtail[:, cols(odd, inner // 2)])
    for i, piece in enumerate(cut_up(mine_end)):
        end[i] = piece
    later = lax.broadcasted_iota(jnp.int32, (span, span), 0)
    earlier = lax.broadcasted_iota(jnp.int32, (span, span), 1)
    score[...] = jnp.where(later >= earlier, dot(c_b, b_t), 0.0)
    decay_swap.wait_recv()

    def relay():
        def part_of(i, _):
            ls = cols(i // 2, LANES)
            mine = ecs[span - 8 : span, cols(odd * half + i // 2, LANES)][7:8, :]
            other = pair_decay[:, ls][7:8, :]
            end_swap(i).wait_recv()
            end_mine = end[i]
            end_other = x_in[i].astype(F32)

            @pl.when(has_prev2)
            def _():
                hand_down(i, c - 2).wait_recv()

            even = odd == 0
            first = g_in[i].astype(F32)
            second = jnp.where(even, mine, other) * first + jnp.where(even, end_mine, end_other)

            @pl.when(has_next2)
            def _():
                after = jnp.where(even, other, mine) * second
                after = after + jnp.where(even, end_other, end_mine)
                g_out[i] = after.astype(BF16)
                hand_down(i, c + 2).start()

            p_out[i] = jnp.where(even, second, first).astype(BF16)
            share(i).start()
            st_in[odd * pieces + i] = jnp.where(even, first, second).astype(BF16)
            return 0

        lax.fori_loop(0, pieces, part_of, 0)

    @pl.when(c < 2)
    def _():
        relay()

    low_row = lax.broadcasted_iota(jnp.int32, (1, LANES), 1) < head_width
    low_head = lax.broadcasted_iota(jnp.int32, (LANES, LANES), 1) < head_width
    for j in range(parts):
        if j == parts // 2:

            @pl.when((c >= 2) & (c < 4))
            def _():
                relay()

        ls = slice(j * LANES, (j + 1) * LANES)
        for r in range(span // LANES):
            rs = slice(r * LANES, (r + 1) * LANES)
            upto = (r + 1) * LANES
            both = []
            for h in (2 * j, 2 * j + 1):
                diff = cs[rs, h : h + 1] - cs_t[h : h + 1, 0:upto]
                weights = score[rs, 0:upto] * jnp.exp(jnp.minimum(diff, 0.0))
                both.append(dot(weights.astype(BF16), xdt[0:upto, ls]))
            skip = jnp.where(low_row, skip_col[2 * j : 2 * j + 1], skip_col[2 * j + 1 : 2 * j + 2])
            yb[rs, ls] = jnp.where(low_head, both[0], both[1]) + skip * xc[rs, ls]

    @pl.when(c >= 4)
    def _():
        relay()

    same = (
        lax.broadcasted_iota(jnp.int32, (2 * LANES, LANES), 0) % LANES // head_width
        == lax.broadcasted_iota(jnp.int32, (2 * LANES, LANES), 1) // head_width
    )
    same = jnp.where(same, 1.0 / head_width, 0.0).astype(BF16)

    def finish_heads(j):
        ls = cols(j, LANES)
        state = st_in[pl.ds(2 * j, 2)].reshape(states, LANES)
        y = yb[:, ls] + ecs[:, ls] * dot(c_b, state)
        mean_sq = dot(jnp.concatenate(split(y * y, 2), axis=1), same)
        normed[:, ls] = (y * lax.rsqrt(mean_sq + 1e-5) * gain[:, ls]).astype(BF16)

    for i in range(half):
        finish_heads(odd * half + i)
    for i in range(half):
        shared(2 * i).wait_recv()
        shared(2 * i + 1).wait_recv()
        finish_heads((1 - odd) * half + i)

    load_out.wait()

    def hop1(j):
        return remote(send1.at[j], recv1.at[j], r1_send.at[j], r1_recv.at[j], c, mate)

    def hop2(j):
        return remote(send2.at[j], recv2.at[j], r2_send.at[j], r2_recv.at[j], c, across)

    def multiply(j):
        prod = dot(normed[...], w_out[:, cols(j, oc)])
        part[...] = prod.reshape(4, rows, oc)
        send1[j, 0] = part[far].astype(BF16)
        send1[j, 1] = part[mate].astype(BF16)
        hop1(j).start()
        own[j, 0] = part[across]
        own[j, 1] = part[t]

    def pass_on(j):
        hop1(j).wait_recv()
        send2[j] = (own[j, 0] + recv1[j, 0].astype(F32)).astype(BF16)
        hop2(j).start()

    for j in range(LAG):
        multiply(j)

    def step(j, _):
        multiply(j)
        pass_on(j - LAG)
        return 0

    lax.fori_loop(LAG, OUT_PARTS, step, 0)
    for j in range(OUT_PARTS - LAG, OUT_PARTS):
        pass_on(j)

    def store(j):
        return pltpu.make_async_copy(staged.at[j], out.at[:, cols(j, oc)], out_sem.at[j])

    def finish(j, _):
        hop2(j).wait_recv()
        total = own[j, 1] + recv1[j, 1].astype(F32) + recv2[j].astype(F32)
        staged[j] = total.astype(BF16)
        store(j).start()
        return 0

    lax.fori_loop(0, OUT_PARTS, finish, 0)

    def drain_k(k, _):
        copy_a(k).wait_send()
        copy_b(k).wait_send()
        copy_f(k).wait_send()
        return 0

    lax.fori_loop(0, K_PARTS, drain_k, 0)

    def drain_o(j, _):
        hop1(j).wait_send()
        hop2(j).wait_send()
        store(j).wait()
        return 0

    lax.fori_loop(0, OUT_PARTS, drain_o, 0)

    decay_swap.wait_send()

    def drain_s(i, _):
        end_swap(i).wait_send()
        share(i).wait_send()
        return 0

    lax.fori_loop(0, pieces, drain_s, 0)

    @pl.when(has_next)
    def _():
        conv_send.wait_send()

    @pl.when(has_next2)
    def _():
        def drain_g(i, _):
            hand_down(i, c + 2).wait_send()
            return 0

        lax.fori_loop(0, pieces, drain_g, 0)


def per_device(
    ctx_size, tokens, in_x, in_bc, in_dt, conv_x, conv_bc, dt_bias, a_log, skip_d, norm_gain, out_w
):
    rows, depth = tokens.shape
    span = 4 * rows
    inner = in_x.shape[1]
    wide = inner + in_bc.shape[1]
    states = in_bc.shape[1] // 2
    heads = a_log.shape[0]
    parts = inner // LANES
    half = parts // 2
    oc = depth // OUT_PARTS
    dma = pltpu.SemaphoreType.DMA
    anywhere = pl.BlockSpec(memory_space=pl.ANY)
    return pl.pallas_call(
        functools.partial(layer_kernel, ctx_size),
        out_shape=jax.ShapeDtypeStruct((rows, depth), BF16),
        in_specs=[anywhere] * 11,
        out_specs=anywhere,
        scratch_shapes=[
            pltpu.VMEM((1, heads), F32),
            pltpu.VMEM((1, heads), F32),
            pltpu.VMEM((1, heads), F32),
            pltpu.VMEM((1, inner), F32),
            pltpu.VMEM((OUT_PARTS, rows, oc), BF16),
            pltpu.VMEM((4, rows, depth), BF16),
            pltpu.VMEM((depth, wide), BF16),
            pltpu.VMEM((heads, depth), BF16),
            pltpu.VMEM((inner, depth), BF16),
            pltpu.VMEM((span, wide), F32),
            pltpu.VMEM((heads, span), F32),
            pltpu.VMEM((span + 8, wide), F32),
            pltpu.VMEM((4, wide), F32),
            pltpu.VMEM((span, wide), F32),
            pltpu.VMEM((span, inner), BF16),
            pltpu.VMEM((span, inner), BF16),
            pltpu.VMEM((span, inner), F32),
            pltpu.VMEM((span, span), BF16),
            pltpu.VMEM((parts, 8 * heads, 3 * LANES), BF16),
            pltpu.VMEM((span, inner), F32),
            pltpu.VMEM((span, span), F32),
            pltpu.VMEM((2 * half, states // 2, LANES), F32),
            pltpu.VMEM((2 * parts, states // 2, LANES), BF16),
            pltpu.VMEM((2 * half, states // 2, LANES), BF16),
            pltpu.VMEM((2 * half, states // 2, LANES), BF16),
            pltpu.VMEM((2 * half, states // 2, LANES), BF16),
            pltpu.VMEM((2 * half, states // 2, LANES), BF16),
            pltpu.VMEM((2 * half, states // 2, LANES), BF16),
            pltpu.VMEM((8, inner // 2), F32),
            pltpu.VMEM((span, inner), BF16),
            pltpu.VMEM((4, rows, oc), F32),
            pltpu.VMEM((OUT_PARTS, 2, rows, oc), F32),
            pltpu.VMEM((OUT_PARTS, 2, rows, oc), BF16),
            pltpu.VMEM((OUT_PARTS, 2, rows, oc), BF16),
            pltpu.VMEM((OUT_PARTS, rows, oc), BF16),
            pltpu.VMEM((OUT_PARTS, rows, oc), BF16),
            dma((6,)),
            dma((OUT_PARTS,)),
            dma((3, K_PARTS)),
            dma(()),
            dma((K_PARTS,)),
            dma((K_PARTS,)),
            dma((K_PARTS,)),
            dma((K_PARTS,)),
            dma((K_PARTS,)),
            dma((K_PARTS,)),
            dma((2,)),
            dma((2,)),
            dma((2 * half,)),
            dma((2 * half,)),
            dma((2 * half,)),
            dma((2 * half,)),
            dma((2 * half,)),
            dma((2 * half,)),
            dma((OUT_PARTS,)),
            dma((OUT_PARTS,)),
            dma((OUT_PARTS,)),
            dma((OUT_PARTS,)),
        ],
        compiler_params=pltpu.CompilerParams(
            collective_id=0, has_side_effects=True, vmem_limit_bytes=56 * 2**20
        ),
    )(
        tokens,
        in_x,
        in_bc,
        in_dt.T,
        out_w,
        conv_x,
        conv_bc,
        dt_bias.reshape(1, heads),
        a_log.reshape(1, heads),
        skip_d.reshape(1, heads),
        norm_gain.reshape(1, inner),
    )


def solution(mesh):
    return jax.shard_map(
        functools.partial(per_device, mesh.shape["ctx"]),
        mesh=mesh,
        in_specs=(
            P(("ctx", "tp"), None),
            P(None, "tp"),
            P(),
            P(None, "tp"),
            P(None, "tp"),
            P(),
            P("tp"),
            P("tp"),
            P("tp"),
            P("tp"),
            P("tp", None),
        ),
        out_specs=P(("ctx", "tp"), None),
        check_vma=False,
    )
```

```python
import functools

import jax
import jax.numpy as jnp
from jax import lax
from jax.experimental import pallas as pl
from jax.experimental.pallas import tpu as pltpu
from jax.sharding import PartitionSpec as P

MESH = pl.DeviceIdType.MESH
F32 = jnp.float32
BF16 = jnp.bfloat16
K_PARTS = 8
OUT_PARTS = 16
TILE = 256
LANES = 128


def dot(a, b):
    return jnp.dot(a, b, preferred_element_type=F32)


def split(v, parts):
    terms = []
    for _ in range(parts):
        term = v.astype(BF16)
        terms.append(term)
        v = v - term.astype(F32)
    return terms


def layer_kernel(
    ctx_size,
    tokens,
    in_x,
    in_bc,
    in_dt,
    out_w,
    conv_x,
    conv_bc,
    dt_bias_in,
    a_log_in,
    skip_d_in,
    gain_in,
    out,
    dt_bias,
    a_log,
    skip_d,
    gain,
    staged,
    gath,
    w_in,
    w_dt,
    w_out,
    acc,
    acc_dt,
    ext,
    taps,
    xc,
    xdt,
    xtail,
    ecs,
    tri_t,
    spread,
    yb,
    score,
    end,
    st_in,
    x_out,
    x_in,
    g_out,
    g_in,
    p_out,
    pair_decay,
    normed,
    ordered,
    own,
    send1,
    recv1,
    send2,
    recv2,
    small_sem,
    out_sem,
    load_sem,
    tok_sem,
    a_send,
    a_recv,
    b_send,
    b_recv,
    f_send,
    f_recv,
    conv_sem,
    d_sem,
    x_send,
    x_recv,
    g_send,
    g_recv,
    p_send,
    p_recv,
    r1_send,
    r1_recv,
    r2_send,
    r2_recv,
):
    c = lax.axis_index("ctx")
    t = lax.axis_index("tp")
    mate = t + 1 - 2 * (t % 2)
    across = (t + 2) % 4
    far = (mate + 2) % 4
    rows, depth = tokens.shape
    span = 4 * rows
    inner = in_x.shape[1]
    bc = in_bc.shape[1]
    wide = inner + bc
    states = bc // 2
    heads = dt_bias_in.shape[1]
    kc = depth // K_PARTS
    oc = depth // OUT_PARTS
    has_prev = c > 0
    has_next = c < ctx_size - 1
    has_prev2 = c > 1
    has_next2 = c < ctx_size - 2
    odd = c % 2
    pair = c + 1 - 2 * odd
    parts = inner // LANES
    half = parts // 2

    def cols(i, size):
        return pl.ds(pl.multiple_of(i * size, size), size)

    def load(k):
        ks = cols(k, kc)
        return (
            pltpu.make_async_copy(in_x.at[ks, :], w_in.at[ks, 0:inner], load_sem.at[0, k]),
            pltpu.make_async_copy(in_bc.at[ks, :], w_in.at[ks, inner:wide], load_sem.at[1, k]),
        )

    load_dt = pltpu.make_async_copy(in_dt, w_dt, load_sem.at[2, 0])
    load_out = pltpu.make_async_copy(out_w, w_out, load_sem.at[2, 1])
    load_tok = pltpu.make_async_copy(tokens, gath.at[t], tok_sem)

    def remote(src, dst, send, recv, cc, tt):
        return pltpu.make_async_remote_copy(
            src_ref=src,
            dst_ref=dst,
            send_sem=send,
            recv_sem=recv,
            device_id=(cc, tt),
            device_id_type=MESH,
        )

    def copy_a(k):
        ks = cols(k, kc)
        return remote(
            tokens.at[:, ks], gath.at[t, :, ks], a_send.at[k], a_recv.at[k], c, across
        )

    def copy_b(k):
        ks = cols(k, kc)
        return remote(tokens.at[:, ks], gath.at[t, :, ks], b_send.at[k], b_recv.at[k], c, mate)

    def copy_f(k):
        ks = cols(k, kc)
        return remote(
            gath.at[across, :, ks], gath.at[across, :, ks], f_send.at[k], f_recv.at[k], c, mate
        )

    def got(block, k, send, recv):
        ks = cols(k, kc)
        return remote(
            gath.at[block, :, ks], gath.at[block, :, ks], send.at[k], recv.at[k], c, mate
        )

    barrier = pltpu.get_barrier_semaphore()
    for tt in (mate, across):
        pl.semaphore_signal(barrier, inc=1, device_id=(c, tt), device_id_type=MESH)

    @pl.when(has_prev)
    def _():
        pl.semaphore_signal(barrier, inc=1, device_id=(c - 1, t), device_id_type=MESH)

    @pl.when(has_next)
    def _():
        pl.semaphore_signal(barrier, inc=1, device_id=(c + 1, t), device_id_type=MESH)

    @pl.when(has_prev2)
    def _():
        pl.semaphore_signal(barrier, inc=1, device_id=(c - 2, t), device_id_type=MESH)

    @pl.when(has_next2)
    def _():
        pl.semaphore_signal(barrier, inc=1, device_id=(c + 2, t), device_id_type=MESH)

    load_tok.start()
    load_dt.start()
    small = [
        pltpu.make_async_copy(src, dst, small_sem.at[i])
        for i, (src, dst) in enumerate(
            (
                (conv_x, taps.at[:, 0:inner]),
                (conv_bc, taps.at[:, inner:wide]),
                (dt_bias_in, dt_bias),
                (a_log_in, a_log),
                (skip_d_in, skip_d),
                (gain_in, gain),
            )
        )
    ]
    for copy in small:
        copy.start()
    for k in range(K_PARTS):
        for copy in load(k):
            copy.start()

    peers = 2
    for flag in (has_prev, has_next, has_prev2, has_next2):
        peers = peers + jnp.where(flag, 1, 0)
    pl.semaphore_wait(barrier, peers)

    for k in range(K_PARTS):
        copy_a(k).start()
    for k in range(K_PARTS):
        copy_b(k).start()

    acc[...] = jnp.zeros_like(acc)
    acc_dt[...] = jnp.zeros_like(acc_dt)

    @pl.when(c == 0)
    def _():
        ext[0:8, :] = jnp.zeros((8, wide), F32)

    @pl.when(c < 2)
    def _():
        g_in[...] = jnp.zeros_like(g_in)

    head_width = inner // heads
    fields = 8 * heads
    earlier = lax.broadcasted_iota(jnp.int32, (span, span), 0)
    later = lax.broadcasted_iota(jnp.int32, (span, span), 1)
    tri_t[...] = jnp.where(later >= earlier, 1.0, 0.0).astype(BF16)
    field = lax.broadcasted_iota(jnp.int32, (fields, 3 * LANES), 0)
    lane = lax.broadcasted_iota(jnp.int32, (fields, 3 * LANES), 1)
    for j in range(parts):
        head = (lane % LANES + j * LANES) // head_width
        hit = (field % heads == head) & (field // (2 * heads) == lane // LANES)
        spread[j] = jnp.where(hit, 1.0, 0.0).astype(BF16)
    eye = lax.broadcasted_iota(jnp.int32, (heads, heads), 0) == lax.broadcasted_iota(
        jnp.int32, (heads, heads), 1
    )

    def upright(row):
        return jnp.sum(jnp.where(eye, row, 0.0), axis=1, keepdims=True)

    for copy in small:
        copy.wait()
    bias = upright(dt_bias[...])
    rate = -jnp.exp(upright(a_log[...]))
    skip_col = jnp.broadcast_to(upright(skip_d[...]), (heads, LANES))

    load_tok.wait()
    load_dt.wait()

    def forward(k):
        got(across, k, a_send, a_recv).wait_recv()
        copy_f(k).start()

    def project(k):
        ks = cols(k, kc)
        got(mate, k, b_send, b_recv).wait_recv()
        for copy in load(k):
            copy.wait()
        got(far, k, f_send, f_recv).wait_recv()
        lhs = gath[:, :, ks].reshape(span, kc)
        acc_dt[...] += lax.dot_general(
            w_dt[:, ks], lhs, (((1,), (1,)), ((), ())), preferred_element_type=F32
        )

        for n in range(wide // TILE):
            ns = slice(n * TILE, (n + 1) * TILE)
            acc[:, ns] += dot(lhs, w_in[ks, ns])

    def gather_step(k, _):
        forward(k)
        project(k - 1)
        return 0

    forward(0)
    lax.fori_loop(1, K_PARTS, gather_step, 0)
    project(K_PARTS - 1)
    load_out.start()

    ext[span : span + 8, :] = acc[span - 8 : span, :].astype(BF16).astype(F32)
    conv_send = remote(
        ext.at[span : span + 8, :], ext.at[0:8, :], conv_sem.at[0], conv_sem.at[1], c + 1, t
    )
    conv_recv = remote(
        ext.at[span : span + 8, :], ext.at[0:8, :], conv_sem.at[0], conv_sem.at[1], c - 1, t
    )

    @pl.when(has_next)
    def _():
        conv_send.start()

    for n in range(wide // TILE):
        ns = slice(n * TILE, (n + 1) * TILE)
        ext[8:span, ns] = acc[0 : span - 8, ns].astype(BF16).astype(F32)

    v = acc_dt[...] + bias
    dt = jnp.maximum(v, 0.0) + jnp.log1p(jnp.exp(-jnp.abs(v)))
    sums = dot(jnp.concatenate(split(rate * dt, 3), axis=0), tri_t[...])
    cs_t = sums[0:heads] + sums[heads : 2 * heads] + sums[2 * heads :]
    tail = jnp.exp(cs_t[:, span - 1 : span] - cs_t)
    rows_of = []
    for quantity in (dt, dt * tail, jnp.exp(cs_t)):
        rows_of += [term.astype(F32) for term in split(quantity, 2)]
    cs_wide = jnp.concatenate(rows_of + [cs_t, jnp.zeros_like(cs_t)], axis=0).T
    cs = cs_wide[:, 6 * heads : 7 * heads]
    wide_b = cs_wide.astype(BF16)
    for j in range(parts):
        ls = slice(j * LANES, (j + 1) * LANES)
        ecs[span - 8 : span, ls] = dot(wide_b[span - 16 : span], spread[j])[8:16, 2 * LANES :]

    theirs = cols(1 - odd, inner // 2)
    decay_swap = remote(
        ecs.at[span - 8 : span, theirs], pair_decay, d_sem.at[0], d_sem.at[1], pair, t
    )
    decay_swap.start()

    step_rows = 64

    def conv(ns, r, scales):
        rs = slice(r, r + step_rows)
        total = taps[0:1, ns] * ext[5 + r : 5 + r + step_rows, ns]
        for k in range(1, 4):
            total = total + taps[k : k + 1, ns] * ext[5 + k + r : 5 + k + r + step_rows, ns]
        x = 0.5 * total
        x = x * jnp.tanh(x) + x
        xc[rs, ns] = x
        if scales is not None:
            xdt[rs, ns] = (x * scales[rs, 0:LANES]).astype(BF16)
            xtail[rs, ns] = (x * scales[rs, LANES : 2 * LANES]).astype(BF16)
            upto = min(r + step_rows, span - 8)
            ecs[r:upto, ns] = scales[r:upto, 2 * LANES :]

    bc_tiles = [slice(n, n + LANES) for n in range(inner, wide, LANES)]
    for ns in bc_tiles:
        for r in range(step_rows, span, step_rows):
            conv(ns, r, None)
    tiles = []
    for i in range(half):
        n = (1 - odd) * half + i
        scales = dot(wide_b, spread[n])
        tiles.append((cols(n, LANES), scales))
        for r in range(step_rows, span, step_rows):
            conv(cols(n, LANES), r, scales)

    @pl.when(has_prev)
    def _():
        conv_recv.wait_recv()

    for ns in bc_tiles:
        conv(ns, 0, None)
    for ns, scales in tiles:
        conv(ns, 0, scales)

    b_t = xc[:, inner : inner + states].T.astype(BF16)
    c_b = xc[:, inner + states : wide].astype(BF16)

    def end_swap(i):
        return remote(x_out.at[i], x_in.at[i], x_send.at[i], x_recv.at[i], pair, t)

    def hand_down(i, cc):
        return remote(g_out.at[i], g_in.at[i], g_send.at[i], g_recv.at[i], cc, t)

    def share(i):
        j = odd * 2 * half + i
        return remote(p_out.at[i], st_in.at[j], p_send.at[i], p_recv.at[i], pair, t)

    def shared(i):
        j = (1 - odd) * 2 * half + i
        return remote(p_out.at[i], st_in.at[j], p_send.at[i], p_recv.at[i], pair, t)

    theirs_end = dot(b_t, xtail[:, theirs]).astype(BF16)
    low = states // 2
    pieces = 2 * half

    def cut_up(whole):
        for i in range(pieces):
            yield whole[(i % 2) * low : (i % 2 + 1) * low, i // 2 * LANES : (i // 2 + 1) * LANES]

    for i, piece in enumerate(cut_up(theirs_end)):
        x_out[i] = piece
        end_swap(i).start()
    for i in range(half):
        n = odd * half + i
        scales = dot(wide_b, spread[n])
        for r in range(0, span, step_rows):
            conv(cols(n, LANES), r, scales)
    mine_end = dot(b_t, xtail[:, cols(odd, inner // 2)])
    for i, piece in enumerate(cut_up(mine_end)):
        end[i] = piece
    later = lax.broadcasted_iota(jnp.int32, (span, span), 0)
    earlier = lax.broadcasted_iota(jnp.int32, (span, span), 1)
    score[...] = jnp.where(later >= earlier, dot(c_b, b_t), 0.0)
    decay_swap.wait_recv()

    def relay_piece(i, _):
        ls = cols(i // 2, LANES)
        mine = ecs[span - 8 : span, cols(odd * half + i // 2, LANES)][7:8, :]
        other = pair_decay[:, ls][7:8, :]
        end_swap(i).wait_recv()
        end_mine = end[i]
        end_other = x_in[i].astype(F32)

        @pl.when(has_prev2)
        def _():
            hand_down(i, c - 2).wait_recv()

        even = odd == 0
        first = g_in[i].astype(F32)
        second = jnp.where(even, mine, other) * first + jnp.where(even, end_mine, end_other)

        @pl.when(has_next2)
        def _():
            after = jnp.where(even, other, mine) * second
            after = after + jnp.where(even, end_other, end_mine)
            g_out[i] = after.astype(BF16)
            hand_down(i, c + 2).start()

        p_out[i] = jnp.where(even, second, first).astype(BF16)
        share(i).start()
        st_in[odd * pieces + i] = jnp.where(even, first, second).astype(BF16)
        return 0

    def relay():
        lax.fori_loop(0, pieces, relay_piece, 0)

    @pl.when(c < 2)
    def _():
        relay()

    low_row = lax.broadcasted_iota(jnp.int32, (1, LANES), 1) < head_width
    low_head = lax.broadcasted_iota(jnp.int32, (LANES, LANES), 1) < head_width
    for j in range(parts):
        if j == parts // 2:

            @pl.when((c >= 2) & (c < 4))
            def _():
                relay()

        ls = slice(j * LANES, (j + 1) * LANES)
        for r in range(span // LANES):
            rs = slice(r * LANES, (r + 1) * LANES)
            upto = (r + 1) * LANES
            both = []
            for h in (2 * j, 2 * j + 1):
                diff = cs[rs, h : h + 1] - cs_t[h : h + 1, 0:upto]
                weights = score[rs, 0:upto] * jnp.exp(jnp.minimum(diff, 0.0))
                both.append(dot(weights.astype(BF16), xdt[0:upto, ls]))
            skip = jnp.where(low_row, skip_col[2 * j : 2 * j + 1], skip_col[2 * j + 1 : 2 * j + 2])
            yb[rs, ls] = jnp.where(low_head, both[0], both[1]) + skip * xc[rs, ls]

    same = (
        lax.broadcasted_iota(jnp.int32, (2 * LANES, LANES), 0) % LANES // head_width
        == lax.broadcasted_iota(jnp.int32, (2 * LANES, LANES), 1) // head_width
    )
    same = jnp.where(same, 1.0 / head_width, 0.0).astype(BF16)

    def finish_heads(j):
        ls = cols(j, LANES)
        state = st_in[pl.ds(2 * j, 2)].reshape(states, LANES)
        y = yb[:, ls] + ecs[:, ls] * dot(c_b, state)
        mean_sq = dot(jnp.concatenate(split(y * y, 2), axis=1), same)
        normed[:, ls] = (y * lax.rsqrt(mean_sq + 1e-5) * gain[:, ls]).astype(BF16)

    @pl.when((c >= 4) & has_next2)
    def _():
        relay()

    at_end = (c >= 4) & (c >= ctx_size - 2)

    @pl.when(at_end)
    def _():
        def tile_of(i, _):
            relay_piece(2 * i, 0)
            relay_piece(2 * i + 1, 0)
            finish_heads(odd * half + i)
            return 0

        lax.fori_loop(0, half, tile_of, 0)


    @pl.when(jnp.logical_not(at_end))
    def _():
        for i in range(half):
            finish_heads(odd * half + i)

    for i in range(half):
        shared(2 * i).wait_recv()
        shared(2 * i + 1).wait_recv()
        finish_heads((1 - odd) * half + i)

    load_out.wait()

    def hop1(j):
        return remote(send1.at[j], recv1.at[j], r1_send.at[j], r1_recv.at[j], c, mate)

    def hop2(j):
        return remote(send2.at[j], recv2.at[j], r2_send.at[j], r2_recv.at[j], c, across)

    def block(b):
        return normed[pl.ds(pl.multiple_of(b * rows, rows), rows), :]

    for at, b in enumerate((far, mate, across, t)):
        ordered[at * rows : (at + 1) * rows, :] = block(b)

    def multiply(j):
        prod = dot(ordered[...], w_out[:, cols(j, 2 * oc)])
        for u in range(2):
            cut_at = slice(u * oc, (u + 1) * oc)
            out_rows = prod[: 2 * rows, cut_at].astype(BF16)
            send1[2 * j + u] = out_rows.reshape(2, rows, oc)
            hop1(2 * j + u).start()
        for u in range(2):
            own[2 * j + u] = prod[2 * rows :, u * oc : (u + 1) * oc].reshape(2, rows, oc)

    def pass_on(j):
        hop1(j).wait_recv()
        send2[j] = (own[j, 0] + recv1[j, 0].astype(F32)).astype(BF16)
        hop2(j).start()

    multiply(0)

    def step(j, _):
        multiply(j)
        pass_on(2 * j - 2)
        pass_on(2 * j - 1)
        return 0

    lax.fori_loop(1, OUT_PARTS // 2, step, 0)
    pass_on(OUT_PARTS - 2)
    pass_on(OUT_PARTS - 1)

    def store(j):
        return pltpu.make_async_copy(staged.at[j], out.at[:, cols(j, oc)], out_sem.at[j])

    def finish(j, _):
        hop2(j).wait_recv()
        total = own[j, 1] + recv1[j, 1].astype(F32) + recv2[j].astype(F32)
        staged[j] = total.astype(BF16)
        store(j).start()
        return 0

    lax.fori_loop(0, OUT_PARTS, finish, 0)

    def drain_k(k, _):
        copy_a(k).wait_send()
        copy_b(k).wait_send()
        copy_f(k).wait_send()
        return 0

    lax.fori_loop(0, K_PARTS, drain_k, 0)

    def drain_o(j, _):
        hop1(j).wait_send()
        hop2(j).wait_send()
        store(j).wait()
        return 0

    lax.fori_loop(0, OUT_PARTS, drain_o, 0)

    decay_swap.wait_send()

    def drain_s(i, _):
        end_swap(i).wait_send()
        share(i).wait_send()
        return 0

    lax.fori_loop(0, pieces, drain_s, 0)

    @pl.when(has_next)
    def _():
        conv_send.wait_send()

    @pl.when(has_next2)
    def _():
        def drain_g(i, _):
            hand_down(i, c + 2).wait_send()
            return 0

        lax.fori_loop(0, pieces, drain_g, 0)


def per_device(
    ctx_size, tokens, in_x, in_bc, in_dt, conv_x, conv_bc, dt_bias, a_log, skip_d, norm_gain, out_w
):
    rows, depth = tokens.shape
    span = 4 * rows
    inner = in_x.shape[1]
    wide = inner + in_bc.shape[1]
    states = in_bc.shape[1] // 2
    heads = a_log.shape[0]
    parts = inner // LANES
    half = parts // 2
    oc = depth // OUT_PARTS
    dma = pltpu.SemaphoreType.DMA
    anywhere = pl.BlockSpec(memory_space=pl.ANY)
    return pl.pallas_call(
        functools.partial(layer_kernel, ctx_size),
        out_shape=jax.ShapeDtypeStruct((rows, depth), BF16),
        in_specs=[anywhere] * 11,
        out_specs=anywhere,
        scratch_shapes=[
            pltpu.VMEM((1, heads), F32),
            pltpu.VMEM((1, heads), F32),
            pltpu.VMEM((1, heads), F32),
            pltpu.VMEM((1, inner), F32),
            pltpu.VMEM((OUT_PARTS, rows, oc), BF16),
            pltpu.VMEM((4, rows, depth), BF16),
            pltpu.VMEM((depth, wide), BF16),
            pltpu.VMEM((heads, depth), BF16),
            pltpu.VMEM((inner, depth), BF16),
            pltpu.VMEM((span, wide), F32),
            pltpu.VMEM((heads, span), F32),
            pltpu.VMEM((span + 8, wide), F32),
            pltpu.VMEM((4, wide), F32),
            pltpu.VMEM((span, wide), F32),
            pltpu.VMEM((span, inner), BF16),
            pltpu.VMEM((span, inner), BF16),
            pltpu.VMEM((span, inner), F32),
            pltpu.VMEM((span, span), BF16),
            pltpu.VMEM((parts, 8 * heads, 3 * LANES), BF16),
            pltpu.VMEM((span, inner), F32),
            pltpu.VMEM((span, span), F32),
            pltpu.VMEM((2 * half, states // 2, LANES), F32),
            pltpu.VMEM((2 * parts, states // 2, LANES), BF16),
            pltpu.VMEM((2 * half, states // 2, LANES), BF16),
            pltpu.VMEM((2 * half, states // 2, LANES), BF16),
            pltpu.VMEM((2 * half, states // 2, LANES), BF16),
            pltpu.VMEM((2 * half, states // 2, LANES), BF16),
            pltpu.VMEM((2 * half, states // 2, LANES), BF16),
            pltpu.VMEM((8, inner // 2), F32),
            pltpu.VMEM((span, inner), BF16),
            pltpu.VMEM((span, inner), BF16),
            pltpu.VMEM((OUT_PARTS, 2, rows, oc), F32),
            pltpu.VMEM((OUT_PARTS, 2, rows, oc), BF16),
            pltpu.VMEM((OUT_PARTS, 2, rows, oc), BF16),
            pltpu.VMEM((OUT_PARTS, rows, oc), BF16),
            pltpu.VMEM((OUT_PARTS, rows, oc), BF16),
            dma((6,)),
            dma((OUT_PARTS,)),
            dma((3, K_PARTS)),
            dma(()),
            dma((K_PARTS,)),
            dma((K_PARTS,)),
            dma((K_PARTS,)),
            dma((K_PARTS,)),
            dma((K_PARTS,)),
            dma((K_PARTS,)),
            dma((2,)),
            dma((2,)),
            dma((2 * half,)),
            dma((2 * half,)),
            dma((2 * half,)),
            dma((2 * half,)),
            dma((2 * half,)),
            dma((2 * half,)),
            dma((OUT_PARTS,)),
            dma((OUT_PARTS,)),
            dma((OUT_PARTS,)),
            dma((OUT_PARTS,)),
        ],
        compiler_params=pltpu.CompilerParams(
            collective_id=0, has_side_effects=True, vmem_limit_bytes=56 * 2**20
        ),
    )(
        tokens,
        in_x,
        in_bc,
        in_dt.T,
        out_w,
        conv_x,
        conv_bc,
        dt_bias.reshape(1, heads),
        a_log.reshape(1, heads),
        skip_d.reshape(1, heads),
        norm_gain.reshape(1, inner),
    )


def solution(mesh):
    return jax.shard_map(
        functools.partial(per_device, mesh.shape["ctx"]),
        mesh=mesh,
        in_specs=(
            P(("ctx", "tp"), None),
            P(None, "tp"),
            P(),
            P(None, "tp"),
            P(None, "tp"),
            P(),
            P("tp"),
            P("tp"),
            P("tp"),
            P("tp"),
            P("tp", None),
        ),
        out_specs=P(("ctx", "tp"), None),
        check_vma=False,
    )
```

```python
import functools

import jax
import jax.numpy as jnp
from jax import lax
from jax.experimental import pallas as pl
from jax.experimental.pallas import tpu as pltpu
from jax.sharding import PartitionSpec as P

MESH = pl.DeviceIdType.MESH
F32 = jnp.float32
BF16 = jnp.bfloat16
K_PARTS = 8
OUT_PARTS = 16
TILE = 256
LANES = 128


def dot(a, b):
    return jnp.dot(a, b, preferred_element_type=F32)


def split(v, parts):
    terms = []
    for _ in range(parts):
        term = v.astype(BF16)
        terms.append(term)
        v = v - term.astype(F32)
    return terms


def layer_kernel(
    ctx_size,
    tokens,
    in_x,
    in_bc,
    in_dt,
    out_w,
    conv_x,
    conv_bc,
    dt_bias_in,
    a_log_in,
    skip_d_in,
    gain_in,
    out,
    dt_bias,
    a_log,
    skip_d,
    gain,
    staged,
    gath,
    w_in,
    w_dt,
    w_out,
    acc,
    acc_dt,
    ext,
    taps,
    xc,
    xdt,
    xtail,
    ecs,
    tri_t,
    spread,
    yb,
    score,
    end,
    st_in,
    x_out,
    x_in,
    g_out,
    g_in,
    p_out,
    pair_decay,
    normed,
    ordered,
    own,
    send1,
    recv1,
    send2,
    recv2,
    small_sem,
    out_sem,
    load_sem,
    tok_sem,
    a_send,
    a_recv,
    b_send,
    b_recv,
    f_send,
    f_recv,
    conv_sem,
    d_sem,
    x_send,
    x_recv,
    g_send,
    g_recv,
    p_send,
    p_recv,
    r1_send,
    r1_recv,
    r2_send,
    r2_recv,
):
    c = lax.axis_index("ctx")
    t = lax.axis_index("tp")
    mate = t + 1 - 2 * (t % 2)
    across = (t + 2) % 4
    far = (mate + 2) % 4
    rows, depth = tokens.shape
    span = 4 * rows
    inner = in_x.shape[1]
    bc = in_bc.shape[1]
    wide = inner + bc
    states = bc // 2
    heads = dt_bias_in.shape[1]
    kc = depth // K_PARTS
    oc = depth // OUT_PARTS
    has_prev = c > 0
    has_next = c < ctx_size - 1
    has_prev2 = c > 1
    has_next2 = c < ctx_size - 2
    odd = c % 2
    pair = c + 1 - 2 * odd
    parts = inner // LANES
    half = parts // 2

    def cols(i, size):
        return pl.ds(pl.multiple_of(i * size, size), size)

    def load(k):
        ks = cols(k, kc)
        return (
            pltpu.make_async_copy(in_x.at[ks, :], w_in.at[ks, 0:inner], load_sem.at[0, k]),
            pltpu.make_async_copy(in_bc.at[ks, :], w_in.at[ks, inner:wide], load_sem.at[1, k]),
        )

    load_dt = pltpu.make_async_copy(in_dt, w_dt, load_sem.at[2, 0])
    load_out = pltpu.make_async_copy(out_w, w_out, load_sem.at[2, 1])
    load_tok = pltpu.make_async_copy(tokens, gath.at[t], tok_sem)

    def remote(src, dst, send, recv, cc, tt):
        return pltpu.make_async_remote_copy(
            src_ref=src,
            dst_ref=dst,
            send_sem=send,
            recv_sem=recv,
            device_id=(cc, tt),
            device_id_type=MESH,
        )

    def copy_a(k):
        ks = cols(k, kc)
        return remote(
            tokens.at[:, ks], gath.at[t, :, ks], a_send.at[k], a_recv.at[k], c, across
        )

    def copy_b(k):
        ks = cols(k, kc)
        return remote(tokens.at[:, ks], gath.at[t, :, ks], b_send.at[k], b_recv.at[k], c, mate)

    def copy_f(k):
        ks = cols(k, kc)
        return remote(
            gath.at[across, :, ks], gath.at[across, :, ks], f_send.at[k], f_recv.at[k], c, mate
        )

    def got(block, k, send, recv):
        ks = cols(k, kc)
        return remote(
            gath.at[block, :, ks], gath.at[block, :, ks], send.at[k], recv.at[k], c, mate
        )

    barrier = pltpu.get_barrier_semaphore()
    for tt in (mate, across):
        pl.semaphore_signal(barrier, inc=1, device_id=(c, tt), device_id_type=MESH)

    @pl.when(has_prev)
    def _():
        pl.semaphore_signal(barrier, inc=1, device_id=(c - 1, t), device_id_type=MESH)

    @pl.when(has_next)
    def _():
        pl.semaphore_signal(barrier, inc=1, device_id=(c + 1, t), device_id_type=MESH)

    @pl.when(has_prev2)
    def _():
        pl.semaphore_signal(barrier, inc=1, device_id=(c - 2, t), device_id_type=MESH)

    @pl.when(has_next2)
    def _():
        pl.semaphore_signal(barrier, inc=1, device_id=(c + 2, t), device_id_type=MESH)

    load_tok.start()
    load_dt.start()
    small = [
        pltpu.make_async_copy(src, dst, small_sem.at[i])
        for i, (src, dst) in enumerate(
            (
                (conv_x, taps.at[:, 0:inner]),
                (conv_bc, taps.at[:, inner:wide]),
                (dt_bias_in, dt_bias),
                (a_log_in, a_log),
                (skip_d_in, skip_d),
                (gain_in, gain),
            )
        )
    ]
    for copy in small:
        copy.start()
    for k in range(K_PARTS):
        for copy in load(k):
            copy.start()

    peers = 2
    for flag in (has_prev, has_next, has_prev2, has_next2):
        peers = peers + jnp.where(flag, 1, 0)
    pl.semaphore_wait(barrier, peers)

    for k in range(K_PARTS):
        copy_a(k).start()
    for k in range(K_PARTS):
        copy_b(k).start()

    acc[...] = jnp.zeros_like(acc)
    acc_dt[...] = jnp.zeros_like(acc_dt)

    @pl.when(c == 0)
    def _():
        ext[0:8, :] = jnp.zeros((8, wide), F32)

    @pl.when(c < 2)
    def _():
        g_in[...] = jnp.zeros_like(g_in)

    head_width = inner // heads
    fields = 8 * heads
    earlier = lax.broadcasted_iota(jnp.int32, (span, span), 0)
    later = lax.broadcasted_iota(jnp.int32, (span, span), 1)
    tri_t[...] = jnp.where(later >= earlier, 1.0, 0.0).astype(BF16)
    field = lax.broadcasted_iota(jnp.int32, (fields, 3 * LANES), 0)
    lane = lax.broadcasted_iota(jnp.int32, (fields, 3 * LANES), 1)
    for j in range(parts):
        head = (lane % LANES + j * LANES) // head_width
        hit = (field % heads == head) & (field // (2 * heads) == lane // LANES)
        spread[j] = jnp.where(hit, 1.0, 0.0).astype(BF16)
    eye = lax.broadcasted_iota(jnp.int32, (heads, heads), 0) == lax.broadcasted_iota(
        jnp.int32, (heads, heads), 1
    )

    def upright(row):
        return jnp.sum(jnp.where(eye, row, 0.0), axis=1, keepdims=True)

    for copy in small:
        copy.wait()
    bias = upright(dt_bias[...])
    rate = -jnp.exp(upright(a_log[...]))
    skip_col = jnp.broadcast_to(upright(skip_d[...]), (heads, LANES))

    load_tok.wait()
    load_dt.wait()

    def forward(k):
        got(across, k, a_send, a_recv).wait_recv()
        copy_f(k).start()

    def project(k):
        ks = cols(k, kc)
        got(mate, k, b_send, b_recv).wait_recv()
        for copy in load(k):
            copy.wait()
        got(far, k, f_send, f_recv).wait_recv()
        lhs = gath[:, :, ks].reshape(span, kc)
        acc_dt[...] += lax.dot_general(
            w_dt[:, ks], lhs, (((1,), (1,)), ((), ())), preferred_element_type=F32
        )

        for n in range(wide // TILE):
            ns = slice(n * TILE, (n + 1) * TILE)
            acc[:, ns] += dot(lhs, w_in[ks, ns])

    def gather_step(k, _):
        forward(k)
        project(k - 1)
        return 0

    forward(0)
    lax.fori_loop(1, K_PARTS, gather_step, 0)
    project(K_PARTS - 1)
    load_out.start()

    ext[span : span + 8, :] = acc[span - 8 : span, :].astype(BF16).astype(F32)
    conv_send = remote(
        ext.at[span : span + 8, :], ext.at[0:8, :], conv_sem.at[0], conv_sem.at[1], c + 1, t
    )
    conv_recv = remote(
        ext.at[span : span + 8, :], ext.at[0:8, :], conv_sem.at[0], conv_sem.at[1], c - 1, t
    )

    @pl.when(has_next)
    def _():
        conv_send.start()

    for n in range(wide // TILE):
        ns = slice(n * TILE, (n + 1) * TILE)
        ext[8:span, ns] = acc[0 : span - 8, ns].astype(BF16).astype(F32)

    v = acc_dt[...] + bias
    dt = jnp.maximum(v, 0.0) + jnp.log1p(jnp.exp(-jnp.abs(v)))
    sums = dot(jnp.concatenate(split(rate * dt, 3), axis=0), tri_t[...])
    cs_t = sums[0:heads] + sums[heads : 2 * heads] + sums[2 * heads :]
    tail = jnp.exp(cs_t[:, span - 1 : span] - cs_t)
    rows_of = []
    for quantity in (dt, dt * tail, jnp.exp(cs_t)):
        rows_of += [term.astype(F32) for term in split(quantity, 2)]
    cs_wide = jnp.concatenate(rows_of + [cs_t, jnp.zeros_like(cs_t)], axis=0).T
    cs = cs_wide[:, 6 * heads : 7 * heads]
    wide_b = cs_wide.astype(BF16)
    for j in range(parts):
        ls = slice(j * LANES, (j + 1) * LANES)
        ecs[span - 8 : span, ls] = dot(wide_b[span - 16 : span], spread[j])[8:16, 2 * LANES :]

    theirs = cols(1 - odd, inner // 2)
    decay_swap = remote(
        ecs.at[span - 8 : span, theirs], pair_decay, d_sem.at[0], d_sem.at[1], pair, t
    )
    decay_swap.start()

    step_rows = 64

    def conv(ns, r, scales):
        rs = slice(r, r + step_rows)
        total = taps[0:1, ns] * ext[5 + r : 5 + r + step_rows, ns]
        for k in range(1, 4):
            total = total + taps[k : k + 1, ns] * ext[5 + k + r : 5 + k + r + step_rows, ns]
        x = 0.5 * total
        x = x * jnp.tanh(x) + x
        xc[rs, ns] = x
        if scales is not None:
            xdt[rs, ns] = (x * scales[rs, 0:LANES]).astype(BF16)
            xtail[rs, ns] = (x * scales[rs, LANES : 2 * LANES]).astype(BF16)
            upto = min(r + step_rows, span - 8)
            ecs[r:upto, ns] = scales[r:upto, 2 * LANES :]

    bc_tiles = [slice(n, n + LANES) for n in range(inner, wide, LANES)]
    for ns in bc_tiles:
        for r in range(step_rows, span, step_rows):
            conv(ns, r, None)
    tiles = []
    for i in range(half):
        n = (1 - odd) * half + i
        scales = dot(wide_b, spread[n])
        tiles.append((cols(n, LANES), scales))
        for r in range(step_rows, span, step_rows):
            conv(cols(n, LANES), r, scales)

    @pl.when(has_prev)
    def _():
        conv_recv.wait_recv()

    for ns in bc_tiles:
        conv(ns, 0, None)
    for ns, scales in tiles:
        conv(ns, 0, scales)

    b_t = xc[:, inner : inner + states].T.astype(BF16)
    c_b = xc[:, inner + states : wide].astype(BF16)

    def end_swap(i):
        return remote(x_out.at[i], x_in.at[i], x_send.at[i], x_recv.at[i], pair, t)

    def hand_down(i, cc):
        return remote(g_out.at[i], g_in.at[i], g_send.at[i], g_recv.at[i], cc, t)

    def share(i):
        j = odd * 2 * half + i
        return remote(p_out.at[i], st_in.at[j], p_send.at[i], p_recv.at[i], pair, t)

    def shared(i):
        j = (1 - odd) * 2 * half + i
        return remote(p_out.at[i], st_in.at[j], p_send.at[i], p_recv.at[i], pair, t)

    theirs_end = dot(b_t, xtail[:, theirs]).astype(BF16)
    low = states // 2
    pieces = 2 * half

    def cut_up(whole):
        for i in range(pieces):
            yield whole[(i % 2) * low : (i % 2 + 1) * low, i // 2 * LANES : (i // 2 + 1) * LANES]

    for i, piece in enumerate(cut_up(theirs_end)):
        x_out[i] = piece
        end_swap(i).start()
    for i in range(half):
        n = odd * half + i
        scales = dot(wide_b, spread[n])
        for r in range(0, span, step_rows):
            conv(cols(n, LANES), r, scales)
    mine_end = dot(b_t, xtail[:, cols(odd, inner // 2)])
    for i, piece in enumerate(cut_up(mine_end)):
        end[i] = piece
    later = lax.broadcasted_iota(jnp.int32, (span, span), 0)
    earlier = lax.broadcasted_iota(jnp.int32, (span, span), 1)
    score[...] = jnp.where(later >= earlier, dot(c_b, b_t), 0.0)
    decay_swap.wait_recv()

    def relay_piece(i, _):
        ls = cols(i // 2, LANES)
        mine = ecs[span - 8 : span, cols(odd * half + i // 2, LANES)][7:8, :]
        other = pair_decay[:, ls][7:8, :]
        end_swap(i).wait_recv()
        end_mine = end[i]
        end_other = x_in[i].astype(F32)

        @pl.when(has_prev2)
        def _():
            hand_down(i, c - 2).wait_recv()

        even = odd == 0
        first = g_in[i].astype(F32)
        second = jnp.where(even, mine, other) * first + jnp.where(even, end_mine, end_other)

        @pl.when(has_next2)
        def _():
            after = jnp.where(even, other, mine) * second
            after = after + jnp.where(even, end_other, end_mine)
            g_out[i] = after.astype(BF16)
            hand_down(i, c + 2).start()

        p_out[i] = jnp.where(even, second, first).astype(BF16)
        share(i).start()
        st_in[odd * pieces + i] = jnp.where(even, first, second).astype(BF16)
        return 0

    def relay():
        lax.fori_loop(0, pieces, relay_piece, 0, unroll=4)

    @pl.when(c < 2)
    def _():
        relay()

    low_row = lax.broadcasted_iota(jnp.int32, (1, LANES), 1) < head_width
    low_head = lax.broadcasted_iota(jnp.int32, (LANES, LANES), 1) < head_width
    for j in range(parts):
        if j == parts // 2:

            @pl.when((c >= 2) & (c < 4))
            def _():
                relay()

        ls = slice(j * LANES, (j + 1) * LANES)
        for r in range(span // LANES):
            rs = slice(r * LANES, (r + 1) * LANES)
            upto = (r + 1) * LANES
            both = []
            for h in (2 * j, 2 * j + 1):
                diff = cs[rs, h : h + 1] - cs_t[h : h + 1, 0:upto]
                weights = score[rs, 0:upto] * jnp.exp(jnp.minimum(diff, 0.0))
                both.append(dot(weights.astype(BF16), xdt[0:upto, ls]))
            skip = jnp.where(low_row, skip_col[2 * j : 2 * j + 1], skip_col[2 * j + 1 : 2 * j + 2])
            yb[rs, ls] = jnp.where(low_head, both[0], both[1]) + skip * xc[rs, ls]

    same = (
        lax.broadcasted_iota(jnp.int32, (2 * LANES, LANES), 0) % LANES // head_width
        == lax.broadcasted_iota(jnp.int32, (2 * LANES, LANES), 1) // head_width
    )
    same = jnp.where(same, 1.0 / head_width, 0.0).astype(BF16)

    def finish_heads(j):
        ls = cols(j, LANES)
        state = st_in[pl.ds(2 * j, 2)].reshape(states, LANES)
        y = yb[:, ls] + ecs[:, ls] * dot(c_b, state)
        mean_sq = dot(jnp.concatenate(split(y * y, 2), axis=1), same)
        normed[:, ls] = (y * lax.rsqrt(mean_sq + 1e-5) * gain[:, ls]).astype(BF16)

    @pl.when((c >= 4) & has_next2)
    def _():
        relay()

    at_end = (c >= 4) & (c >= ctx_size - 2)

    @pl.when(at_end)
    def _():
        def tile_of(i, _):
            relay_piece(2 * i, 0)
            relay_piece(2 * i + 1, 0)
            finish_heads(odd * half + i)
            return 0

        lax.fori_loop(0, half, tile_of, 0)


    @pl.when(jnp.logical_not(at_end))
    def _():
        for i in range(half):
            finish_heads(odd * half + i)

    for i in range(half):
        shared(2 * i).wait_recv()
        shared(2 * i + 1).wait_recv()
        finish_heads((1 - odd) * half + i)

    load_out.wait()

    def hop1(j):
        return remote(send1.at[j], recv1.at[j], r1_send.at[j], r1_recv.at[j], c, mate)

    def hop2(j):
        return remote(send2.at[j], recv2.at[j], r2_send.at[j], r2_recv.at[j], c, across)

    def block(b):
        return normed[pl.ds(pl.multiple_of(b * rows, rows), rows), :]

    for at, b in enumerate((far, mate, across, t)):
        ordered[at * rows : (at + 1) * rows, :] = block(b)

    def multiply(j):
        prod = dot(ordered[...], w_out[:, cols(j, 2 * oc)])
        for u in range(2):
            cut_at = slice(u * oc, (u + 1) * oc)
            out_rows = prod[: 2 * rows, cut_at].astype(BF16)
            send1[2 * j + u] = out_rows.reshape(2, rows, oc)
            hop1(2 * j + u).start()
        for u in range(2):
            own[2 * j + u] = prod[2 * rows :, u * oc : (u + 1) * oc].reshape(2, rows, oc)

    def pass_on(j):
        hop1(j).wait_recv()
        send2[j] = (own[j, 0] + recv1[j, 0].astype(F32)).astype(BF16)
        hop2(j).start()

    multiply(0)

    def step(j, _):
        multiply(j)
        pass_on(2 * j - 2)
        pass_on(2 * j - 1)
        return 0

    lax.fori_loop(1, OUT_PARTS // 2, step, 0)
    pass_on(OUT_PARTS - 2)
    pass_on(OUT_PARTS - 1)

    def store(j):
        return pltpu.make_async_copy(staged.at[j], out.at[:, cols(j, oc)], out_sem.at[j])

    def finish(j, _):
        hop2(j).wait_recv()
        total = own[j, 1] + recv1[j, 1].astype(F32) + recv2[j].astype(F32)
        staged[j] = total.astype(BF16)
        store(j).start()
        return 0

    lax.fori_loop(0, OUT_PARTS, finish, 0)

    def drain_k(k, _):
        copy_a(k).wait_send()
        copy_b(k).wait_send()
        copy_f(k).wait_send()
        return 0

    lax.fori_loop(0, K_PARTS, drain_k, 0)

    def drain_o(j, _):
        hop1(j).wait_send()
        hop2(j).wait_send()
        store(j).wait()
        return 0

    lax.fori_loop(0, OUT_PARTS, drain_o, 0)

    decay_swap.wait_send()

    def drain_s(i, _):
        end_swap(i).wait_send()
        share(i).wait_send()
        return 0

    lax.fori_loop(0, pieces, drain_s, 0)

    @pl.when(has_next)
    def _():
        conv_send.wait_send()

    @pl.when(has_next2)
    def _():
        def drain_g(i, _):
            hand_down(i, c + 2).wait_send()
            return 0

        lax.fori_loop(0, pieces, drain_g, 0)


def per_device(
    ctx_size, tokens, in_x, in_bc, in_dt, conv_x, conv_bc, dt_bias, a_log, skip_d, norm_gain, out_w
):
    rows, depth = tokens.shape
    span = 4 * rows
    inner = in_x.shape[1]
    wide = inner + in_bc.shape[1]
    states = in_bc.shape[1] // 2
    heads = a_log.shape[0]
    parts = inner // LANES
    half = parts // 2
    oc = depth // OUT_PARTS
    dma = pltpu.SemaphoreType.DMA
    anywhere = pl.BlockSpec(memory_space=pl.ANY)
    return pl.pallas_call(
        functools.partial(layer_kernel, ctx_size),
        out_shape=jax.ShapeDtypeStruct((rows, depth), BF16),
        in_specs=[anywhere] * 11,
        out_specs=anywhere,
        scratch_shapes=[
            pltpu.VMEM((1, heads), F32),
            pltpu.VMEM((1, heads), F32),
            pltpu.VMEM((1, heads), F32),
            pltpu.VMEM((1, inner), F32),
            pltpu.VMEM((OUT_PARTS, rows, oc), BF16),
            pltpu.VMEM((4, rows, depth), BF16),
            pltpu.VMEM((depth, wide), BF16),
            pltpu.VMEM((heads, depth), BF16),
            pltpu.VMEM((inner, depth), BF16),
            pltpu.VMEM((span, wide), F32),
            pltpu.VMEM((heads, span), F32),
            pltpu.VMEM((span + 8, wide), F32),
            pltpu.VMEM((4, wide), F32),
            pltpu.VMEM((span, wide), F32),
            pltpu.VMEM((span, inner), BF16),
            pltpu.VMEM((span, inner), BF16),
            pltpu.VMEM((span, inner), F32),
            pltpu.VMEM((span, span), BF16),
            pltpu.VMEM((parts, 8 * heads, 3 * LANES), BF16),
            pltpu.VMEM((span, inner), F32),
            pltpu.VMEM((span, span), F32),
            pltpu.VMEM((2 * half, states // 2, LANES), F32),
            pltpu.VMEM((2 * parts, states // 2, LANES), BF16),
            pltpu.VMEM((2 * half, states // 2, LANES), BF16),
            pltpu.VMEM((2 * half, states // 2, LANES), BF16),
            pltpu.VMEM((2 * half, states // 2, LANES), BF16),
            pltpu.VMEM((2 * half, states // 2, LANES), BF16),
            pltpu.VMEM((2 * half, states // 2, LANES), BF16),
            pltpu.VMEM((8, inner // 2), F32),
            pltpu.VMEM((span, inner), BF16),
            pltpu.VMEM((span, inner), BF16),
            pltpu.VMEM((OUT_PARTS, 2, rows, oc), F32),
            pltpu.VMEM((OUT_PARTS, 2, rows, oc), BF16),
            pltpu.VMEM((OUT_PARTS, 2, rows, oc), BF16),
            pltpu.VMEM((OUT_PARTS, rows, oc), BF16),
            pltpu.VMEM((OUT_PARTS, rows, oc), BF16),
            dma((6,)),
            dma((OUT_PARTS,)),
            dma((3, K_PARTS)),
            dma(()),
            dma((K_PARTS,)),
            dma((K_PARTS,)),
            dma((K_PARTS,)),
            dma((K_PARTS,)),
            dma((K_PARTS,)),
            dma((K_PARTS,)),
            dma((2,)),
            dma((2,)),
            dma((2 * half,)),
            dma((2 * half,)),
            dma((2 * half,)),
            dma((2 * half,)),
            dma((2 * half,)),
            dma((2 * half,)),
            dma((OUT_PARTS,)),
            dma((OUT_PARTS,)),
            dma((OUT_PARTS,)),
            dma((OUT_PARTS,)),
        ],
        compiler_params=pltpu.CompilerParams(
            collective_id=0, has_side_effects=True, vmem_limit_bytes=56 * 2**20
        ),
    )(
        tokens,
        in_x,
        in_bc,
        in_dt.T,
        out_w,
        conv_x,
        conv_bc,
        dt_bias.reshape(1, heads),
        a_log.reshape(1, heads),
        skip_d.reshape(1, heads),
        norm_gain.reshape(1, inner),
    )


def solution(mesh):
    return jax.shard_map(
        functools.partial(per_device, mesh.shape["ctx"]),
        mesh=mesh,
        in_specs=(
            P(("ctx", "tp"), None),
            P(None, "tp"),
            P(),
            P(None, "tp"),
            P(None, "tp"),
            P(),
            P("tp"),
            P("tp"),
            P("tp"),
            P("tp"),
            P("tp", None),
        ),
        out_specs=P(("ctx", "tp"), None),
        check_vma=False,
    )
```
